768 devices in a mesh: rep: 16 (over x_lo, y), shard: 48 (over x_hi, z, core).
Axes of the slice: x: 4 (x_hi: 2, x_lo: 2; x = x_hi * 2 + x_lo), y: 8, z: 12, core: 2. Of those that a mesh axis runs over, the one named last changes fastest.
Arguments:
- queries: bfloat16 [589824, 512], P(('rep', 'shard')), may hold values from -1.5909903 to 1.5909903
- target_ids: int32 [36864, 16], P(('rep', 'shard')), may hold values from 0 to 511
- negative_ids: int32 [36864, 16], P(('rep', 'shard')), may hold values from 0 to 511
- table_rows: float32 [24576, 512], P('shard'), may hold values from -1.5909903 to 1.5909903
- first_moment: float32 [24576, 512], P('shard'), may hold values from -0.5 to 0.5
- second_moment: float32 [24576], P('shard'), may hold values from 0.001 to 0.1
Outputs:
- new_rows: float32 [24576, 512], P('shard')
- new_first: float32 [24576, 512], P('shard')
- new_second: float32 [24576], P('shard')
- grad_queries: float32 [589824, 512], P(('rep', 'shard'))
The draws below stay inside these ranges and needn't reach their ends.
All inputs are finite; a program needn't handle non-finite values.
Results may differ from the reference program's by a relative error of at most 0.0013.
The reference program's roundings to bfloat16 on the way (of `sent_rows`, `cand`, `coef` and `row_bf`) count: a program that leaves them out, or rounds other values in their place, can miss the bound.
Values may be sent and summed in bfloat16 or wider, within the bound.
A program may use at most 64 MiB of HBM per device.

```python
import math
import jax
import jax.numpy as jnp
from jax import lax

D = 512
UNIQ = 512
TGT_OWN = 16
NEG_OWN = 16
TGT_DEV = 768
NEG_DEV = 768
TOKENS = 589824
ROWS = 24576
N_REP = 16
N_SHARD = 48


def spread(values, key_row, key_col, rows, cols):
    row_scale = jnp.exp(jax.random.uniform(key_row, (rows, 1), jnp.float32, math.log(0.3), math.log(3.0)))
    col_scale = jnp.exp(jax.random.uniform(key_col, (1, cols), jnp.float32, math.log(0.3), math.log(3.0)))
    return values * row_scale * col_scale / math.sqrt(cols)


def draw_queries(key, part):
    key = jax.random.fold_in(key, 11)
    key_row, key_col, key_val = jax.random.split(key, 3)
    values = jnp.clip(jax.random.normal(key_val, (TOKENS, D), jnp.float32), -4.0, 4.0)
    return spread(values, key_row, key_col, TOKENS, D).astype(jnp.bfloat16)


def draw_table_rows(key, part):
    key = jax.random.fold_in(key, 23)
    key_row, key_col, key_val = jax.random.split(key, 3)
    values = jnp.clip(jax.random.normal(key_val, (ROWS, D), jnp.float32), -4.0, 4.0)
    return spread(values, key_row, key_col, ROWS, D)


def with_ends(drawn, stream_key, least, high):
    index_at = [jax.random.randint(jax.random.fold_in(stream_key, axis), (), 0, length) for axis, length in enumerate(drawn.shape)]
    widest = drawn.shape.index(max(drawn.shape))
    neighbour = index_at[:widest] + [(index_at[widest] + 1) % drawn.shape[widest]] + index_at[widest + 1:]
    return drawn.at[tuple(index_at)].set(least).at[tuple(neighbour)].set(high)


def levels(key, dims, cuts, low, largest):
    loudness, own = 1.0, jax.random.fold_in(key, 6)
    for axis_at, parts in cuts:
        draws = jnp.exp(jax.random.uniform(jax.random.fold_in(own, axis_at), (parts,), jnp.float32, low / len(cuts), largest / len(cuts)))
        loudness = loudness * jnp.repeat(draws, dims[axis_at] // parts).reshape([-1 if axis == axis_at else 1 for axis in range(len(dims))])
    return loudness


def gaussian(key, extent, scale, most, pieces=(), kind=jnp.bfloat16):
    array = jax.random.normal(key, extent, jnp.float32) * scale
    if len(pieces) > 0:
        array = levels(key, extent, pieces, -0.22, 0.18) * array
    return jnp.clip(array, min=-most, max=most).astype(kind)


def setup_inputs(seed: int = 0) -> dict:
    keys = jax.random.split(jax.random.key(seed), 7)
    return {
        "queries": draw_queries(jax.random.fold_in(keys[6], 71), 0),
        "target_ids": with_ends(jax.random.randint(keys[1], (N_REP * N_SHARD * N_SHARD, TGT_OWN), 0, UNIQ), jax.random.fold_in(keys[1], 1), 0, UNIQ - 1).astype(jnp.int32),
        "negative_ids": with_ends(jax.random.randint(keys[2], (N_REP * N_SHARD * N_SHARD, NEG_OWN), 0, UNIQ), jax.random.fold_in(keys[2], 1), 0, UNIQ - 1).astype(jnp.int32),
        "table_rows": draw_table_rows(jax.random.fold_in(keys[6], 71), 0),
        "first_moment": gaussian(keys[4], (ROWS, D), 0.1, 0.5, ((0, 48),), jnp.float32),
        "second_moment": jnp.clip(jnp.exp(math.log(0.1) - 4.6051702 * jax.random.uniform(keys[5], (ROWS,), jnp.float32) ** levels(keys[5], (ROWS,), ((0, 48),), -0.2, 0.2)), 0.001, 0.1),
    }


SCALE = 72.0

def unit_rows(values):
    norm = jnp.sqrt(lax.optimization_barrier(jnp.sum(values * values, axis=-1, keepdims=True)) + 1e-06)
    return (values / norm, norm)

def project_back(grad, unit, norm):
    return (grad - unit * lax.optimization_barrier(jnp.sum(unit * grad, axis=-1, keepdims=True))) / norm

def block_terms(block_queries, cand):
    query_unit, query_norm = unit_rows(block_queries.astype(jnp.float32))
    cand_unit, cand_norm = unit_rows(cand.astype(jnp.float32))
    query_bf = query_unit.astype(jnp.bfloat16)
    cand_bf = cand_unit.astype(jnp.bfloat16)
    scores = jnp.dot(query_bf, cand_bf.T, preferred_element_type=jnp.float32) * SCALE
    weights = jnp.exp(scores)
    probs = weights / lax.optimization_barrier(jnp.sum(weights, axis=1, keepdims=True))
    rows_idx = lax.broadcasted_iota(jnp.int32, probs.shape, 0)
    cols_idx = lax.broadcasted_iota(jnp.int32, probs.shape, 1)
    labels = jnp.where(rows_idx == cols_idx, 1.0, 0.0).astype(jnp.float32)
    coef = (probs - labels).astype(jnp.bfloat16)
    query_grad = jnp.dot(coef, cand_bf, preferred_element_type=jnp.float32) * SCALE
    grad_queries = project_back(query_grad, query_unit, query_norm)
    cand_grad = jnp.dot(coef.T, query_bf, preferred_element_type=jnp.float32) * SCALE
    row_grad = project_back(cand_grad, cand_unit, cand_norm)
    row_bf = row_grad.astype(jnp.bfloat16)
    return (grad_queries, row_bf)

def reference(queries, target_ids, negative_ids, table_rows, first_moment, second_moment):
    blocks = N_REP * N_SHARD
    owner_base = (jnp.arange(N_SHARD, dtype=jnp.int32) * UNIQ)[:, None]
    query_blocks = queries.reshape(blocks, TGT_DEV, D)
    target_rows = (target_ids.reshape(blocks, N_SHARD, TGT_OWN) + owner_base[None]).reshape(blocks, TGT_DEV)
    negative_rows = (negative_ids.reshape(blocks, N_SHARD, NEG_OWN) + owner_base[None]).reshape(blocks, NEG_DEV)
    sent_rows = table_rows.astype(jnp.bfloat16)

    def step(grad, item):
        block_queries, tgt, neg = item
        index = jnp.concatenate([tgt, neg]).astype(jnp.int32)
        cand = sent_rows[index]
        grad_queries, row_bf = block_terms(block_queries, cand)
        grad = grad.at[index].add(row_bf.astype(jnp.float32))
        return (grad, grad_queries)
    grad, grad_queries = lax.scan(step, jnp.zeros((ROWS, D), jnp.float32), (query_blocks, target_rows, negative_rows))
    new_first = 0.9 * first_moment + 0.1 * grad
    new_second = 0.999 * second_moment + 0.001 * lax.optimization_barrier(jnp.mean(grad * grad, axis=-1))
    new_rows = table_rows - 0.01 * new_first / (jnp.sqrt(new_second)[:, None] + 1e-08)
    return (new_rows, new_first, new_second, grad_queries.reshape(TOKENS, D))
```

```python
import functools

import jax
import jax.numpy as jnp
from jax import lax
from jax.experimental import pallas as pl
from jax.experimental.pallas import tpu as pltpu
from jax.sharding import PartitionSpec as P

SCALE = 72.0
EPS = 1e-06
CHUNKS = 2
BAND = 8
F32 = jnp.float32
BF16 = jnp.bfloat16
NT = (((1,), (1,)), ((), ()))
TN = (((0,), (0,)), ((), ()))


def iota(shape, axis):
    return lax.broadcasted_iota(jnp.int32, shape, axis)


def push(src, dst, send, recv, axis, peer):
    return pltpu.make_async_remote_copy(
        src_ref=src,
        dst_ref=dst,
        send_sem=send,
        recv_sem=recv,
        device_id={axis: peer},
        device_id_type=pl.DeviceIdType.MESH,
    )


def kernel(
    reps,
    shards,
    per_target,
    ids_ref,
    q_ref,
    table_ref,
    gq_ref,
    grad_ref,
    ids_in,
    table_bf,
    onehot_t,
    outgoing,
    arrived,
    query_unit,
    query_norm,
    query_bf,
    cand_unit,
    cand_norm,
    cand_bf,
    weights,
    coef,
    back,
    came,
    local,
    parts,
    gathered,
    ids_send,
    ids_recv,
    rows_send,
    rows_recv,
    back_send,
    back_recv,
    part_send,
    part_recv,
    full_send,
    full_recv,
    own_sem,
):
    me = lax.axis_index("shard")
    rep = lax.axis_index("rep")
    per_peer = outgoing.shape[1]
    uniq, width = table_bf.shape
    tokens = query_bf.shape[0]
    bands = shards // BAND
    band_rows = BAND * per_peer
    lanes = 128
    packs = band_rows // lanes
    per_pack = lanes // per_peer
    span = width // CHUNKS
    slice_rows = uniq // reps
    my_band = me // BAND

    def to_shards(body):
        def step(k, carry):
            body(lax.rem(me + k, shards))
            return carry

        lax.fori_loop(1, shards, step, 0)

    def to_reps(body):
        def step(k, carry):
            body(lax.rem(rep + k, reps))
            return carry

        lax.fori_loop(1, reps, step, 0)

    barrier = pltpu.get_barrier_semaphore()
    to_shards(
        lambda p: pl.semaphore_signal(
            barrier, inc=1, device_id={"shard": p}, device_id_type=pl.DeviceIdType.MESH
        )
    )
    to_reps(
        lambda p: pl.semaphore_signal(
            barrier, inc=1, device_id={"rep": p}, device_id_type=pl.DeviceIdType.MESH
        )
    )
    table_bf[...] = table_ref[...].astype(BF16)
    pl.semaphore_wait(barrier, shards + reps - 2)

    to_shards(
        lambda p: push(ids_ref.at[p], ids_in.at[me], ids_send, ids_recv, "shard", p).start()
    )
    ids_in[me] = ids_ref[me]

    values = q_ref[...].astype(F32)
    norm = jnp.sqrt(jnp.sum(values * values, axis=-1, keepdims=True) + EPS)
    unit = values / norm
    query_norm[...] = norm
    query_unit[...] = unit
    query_bf[...] = unit.astype(BF16)

    others = pl.ds(0, shards - 1)
    push(ids_in.at[others], ids_in.at[others], ids_send, ids_recv, "shard", me).wait()

    def gather(i, carry):
        band = lax.rem(my_band + i, bands)
        first = band * BAND
        which = iota((1, lanes), 1) // per_peer
        flat = []
        tall = []
        for pack in range(packs):
            row = ids_in[first + pack * per_pack]
            for j in range(1, per_pack):
                row = jnp.where(which == j, ids_in[first + pack * per_pack + j], row)
            flat.append(row)
            tall.append(jnp.transpose(jnp.broadcast_to(row, (lanes, lanes))))
        row = jnp.concatenate(flat, axis=1)
        onehot_t[band] = jnp.where(iota((uniq, band_rows), 0) == row, 1.0, 0.0).astype(BF16)
        column = jnp.concatenate(tall, axis=0)
        column = jnp.concatenate([column] * (uniq // lanes), axis=1)
        onehot = jnp.where(iota((band_rows, uniq), 1) == column, 1.0, 0.0).astype(BF16)
        rows = jnp.dot(onehot, table_bf[...], preferred_element_type=F32).astype(BF16)
        outgoing[pl.ds(first, BAND)] = rows.reshape(BAND, per_peer, width)
        for j in range(BAND):
            peer = first + j

            @pl.when(peer != me)
            def _():
                push(
                    outgoing.at[peer], arrived.at[me], rows_send, rows_recv.at[my_band], "shard", peer
                ).start()

            @pl.when(peer == me)
            def _():
                pltpu.make_async_copy(
                    outgoing.at[peer], arrived.at[me], rows_recv.at[my_band]
                ).start()

        return carry

    lax.fori_loop(0, bands, gather, 0)

    def score(i, total):
        band = lax.rem(my_band + i, bands)
        peers = pl.ds(band * BAND, BAND)
        push(
            arrived.at[peers], arrived.at[peers], rows_send, rows_recv.at[band], "shard", me
        ).wait_recv()
        values = arrived[peers].reshape(band_rows, width).astype(F32)
        norm = jnp.sqrt(jnp.sum(values * values, axis=-1, keepdims=True) + EPS)
        unit = values / norm
        unit_bf = unit.astype(BF16)
        cand_norm[band] = norm
        cand_unit[band] = unit
        cand_bf[band] = unit_bf
        scores = lax.dot_general(unit_bf, query_bf[...], NT, preferred_element_type=F32) * SCALE
        weight = jnp.exp(scores)
        weights[band] = weight
        return total + jnp.sum(weight, axis=0, keepdims=True)

    total = lax.fori_loop(0, bands, score, jnp.zeros((1, tokens), F32))
    share = 1.0 / total

    def send_back(chunk, peer):
        push(
            back.at[chunk, peer],
            came.at[chunk, me],
            back_send,
            back_recv.at[chunk],
            "shard",
            peer,
        ).start()

    def row_grads(i, carry):
        band = lax.rem(my_band + i, bands)
        first = band * BAND
        place = iota((band_rows, 1), 0) + band * band_rows
        slot = lax.rem(place, per_peer)
        target = jnp.where(slot < per_target, place // per_peer * per_target + slot, -1)
        label = jnp.where(iota((band_rows, tokens), 1) == target, 1.0, 0.0)
        coef_band = (weights[band] * share - label).astype(BF16)
        coef[band] = coef_band
        grad = jnp.dot(coef_band, query_bf[...], preferred_element_type=F32) * SCALE
        unit = cand_unit[band]
        grad = (grad - unit * jnp.sum(unit * grad, axis=-1, keepdims=True)) / cand_norm[band]
        grad = grad.astype(BF16)
        for chunk in range(CHUNKS):
            back[chunk, pl.ds(first, BAND)] = grad[:, chunk * span : (chunk + 1) * span].reshape(
                BAND, per_peer, span
            )
        for j in range(BAND):
            peer = first + j

            @pl.when(peer != me)
            def _():
                send_back(0, peer)

        return carry

    lax.fori_loop(0, bands, row_grads, 0)
    for chunk in range(1, CHUNKS):
        to_shards(functools.partial(send_back, chunk))
    for chunk in range(CHUNKS):
        pltpu.make_async_copy(back.at[chunk, me], came.at[chunk, me], back_recv.at[chunk]).start()

    tile = 256 if tokens % 256 == 0 else 128

    def query_grads(i, carry):
        at = pl.ds(pl.multiple_of(i * tile, tile), tile)
        grad = jnp.zeros((tile, width), F32)
        for band in range(bands):
            grad += lax.dot_general(
                coef[band, :, at], cand_bf[band], TN, preferred_element_type=F32
            )
        grad = grad * SCALE
        unit = query_unit[at]
        gq_ref[at] = (grad - unit * jnp.sum(unit * grad, axis=-1, keepdims=True)) / query_norm[at]
        return carry

    lax.fori_loop(0, tokens // tile, query_grads, 0)

    def reduce_chunk(chunk):
        push(
            came.at[chunk], came.at[chunk], back_send, back_recv.at[chunk], "shard", me
        ).wait_recv()
        for half in range(2):
            rows = pl.ds(half * (uniq // 2), uniq // 2)
            grad = jnp.zeros((uniq // 2, span), F32)
            for band in range(bands):
                grad += jnp.dot(
                    onehot_t[band, rows, :],
                    came[chunk, pl.ds(band * BAND, BAND)].reshape(band_rows, span),
                    preferred_element_type=F32,
                )
            local[chunk, pl.ds(half * (reps // 2), reps // 2)] = grad.reshape(
                reps // 2, slice_rows, span
            )
        to_reps(
            lambda p: push(
                local.at[chunk, p], parts.at[chunk, rep], part_send, part_recv.at[chunk], "rep", p
            ).start()
        )

    def share_chunk(chunk):
        other = pl.ds(0, reps - 1)
        push(
            parts.at[chunk, other],
            parts.at[chunk, other],
            part_send,
            part_recv.at[chunk],
            "rep",
            rep,
        ).wait_recv()
        parts[chunk, rep] = local[chunk, rep]
        gathered[chunk, rep] = jnp.sum(parts[chunk], axis=0)
        to_reps(
            lambda p: push(
                gathered.at[chunk, rep],
                gathered.at[chunk, rep],
                full_send,
                full_recv.at[chunk],
                "rep",
                p,
            ).start()
        )

    def finish_chunk(chunk):
        other = pl.ds(0, reps - 1)
        push(
            gathered.at[chunk, other],
            gathered.at[chunk, other],
            full_send,
            full_recv.at[chunk],
            "rep",
            rep,
        ).wait_recv()
        grad_ref[:, chunk * span : (chunk + 1) * span] = gathered[chunk].reshape(uniq, span)

    for chunk in range(CHUNKS):
        reduce_chunk(chunk)
        share_chunk(chunk)
    for chunk in range(CHUNKS):
        finish_chunk(chunk)

    other_rows = pl.ds(0, shards - 1)
    push(
        outgoing.at[other_rows], outgoing.at[other_rows], rows_send, ids_recv, "shard", me
    ).wait_send()
    for chunk in range(CHUNKS):
        other = pl.ds(0, shards - 1)
        push(
            back.at[chunk, other], back.at[chunk, other], back_send, ids_recv, "shard", me
        ).wait_send()
        other = pl.ds(0, reps - 1)
        push(
            local.at[chunk, other], local.at[chunk, other], part_send, ids_recv, "rep", rep
        ).wait_send()
        push(
            gathered.at[chunk, other], gathered.at[chunk, other], full_send, ids_recv, "rep", rep
        ).wait_send()


def adam_rows(rows, first, second, grad):
    new_first = 0.9 * first + 0.1 * grad
    new_second = 0.999 * second + 0.001 * jnp.mean(grad * grad, axis=-1)
    new_rows = rows - 0.01 * new_first / (jnp.sqrt(new_second)[:, None] + 1e-08)
    return (new_rows, new_first, new_second)


def per_device(reps, shards, queries, target_ids, negative_ids, table_rows, first_moment, second_moment):
    tokens, width = queries.shape
    uniq = table_rows.shape[0]
    per_target = target_ids.shape[1]
    per_peer = per_target + negative_ids.shape[1]
    bands = shards // BAND
    band_rows = BAND * per_peer
    cands = shards * per_peer
    span = width // CHUNKS
    ids = jnp.concatenate([target_ids, negative_ids], axis=1)
    ids = jnp.tile(ids, (1, 128 // per_peer))[:, None, :]
    dma = pltpu.SemaphoreType.DMA
    vmem = pl.BlockSpec(memory_space=pltpu.VMEM)
    grad_queries, grad = pl.pallas_call(
        functools.partial(kernel, reps, shards, per_target),
        out_shape=(
            jax.ShapeDtypeStruct((tokens, width), F32),
            jax.ShapeDtypeStruct((uniq, width), F32),
        ),
        in_specs=[vmem] * 3,
        out_specs=(vmem, vmem),
        scratch_shapes=[
            pltpu.VMEM((shards, 1, 128), jnp.int32),
            pltpu.VMEM((uniq, width), BF16),
            pltpu.VMEM((bands, uniq, band_rows), BF16),
            pltpu.VMEM((shards, per_peer, width), BF16),
            pltpu.VMEM((shards, per_peer, width), BF16),
            pltpu.VMEM((tokens, width), F32),
            pltpu.VMEM((tokens, 1), F32),
            pltpu.VMEM((tokens, width), BF16),
            pltpu.VMEM((bands, band_rows, width), F32),
            pltpu.VMEM((bands, band_rows, 1), F32),
            pltpu.VMEM((bands, band_rows, width), BF16),
            pltpu.VMEM((bands, band_rows, tokens), F32),
            pltpu.VMEM((bands, band_rows, tokens), BF16),
            pltpu.VMEM((CHUNKS, shards, per_peer, span), BF16),
            pltpu.VMEM((CHUNKS, shards, per_peer, span), BF16),
            pltpu.VMEM((CHUNKS, reps, uniq // reps, span), F32),
            pltpu.VMEM((CHUNKS, reps, uniq // reps, span), F32),
            pltpu.VMEM((CHUNKS, reps, uniq // reps, span), F32),
            dma,
            dma,
            dma,
            dma((bands,)),
            dma,
            dma((CHUNKS,)),
            dma,
            dma((CHUNKS,)),
            dma,
            dma((CHUNKS,)),
            dma,
        ],
        compiler_params=pltpu.CompilerParams(
            collective_id=0, has_side_effects=True, vmem_limit_bytes=56 * 1024 * 1024
        ),
        cost_estimate=pl.CostEstimate(
            flops=2 * width * (3 * tokens * cands + 2 * uniq * cands),
            bytes_accessed=width * (6 * tokens + 8 * uniq),
            transcendentals=tokens * cands,
        ),
    )(ids, queries, table_rows)
    new_rows, new_first, new_second = adam_rows(table_rows, first_moment, second_moment, grad)
    return (new_rows, new_first, new_second, grad_queries)


def solution(mesh):
    return jax.shard_map(
        functools.partial(per_device, mesh.shape["rep"], mesh.shape["shard"]),
        mesh=mesh,
        in_specs=(
            P(("rep", "shard"), None),
            P(("rep", "shard"), None),
            P(("rep", "shard"), None),
            P("shard", None),
            P("shard", None),
            P("shard"),
        ),
        out_specs=(P("shard", None), P("shard", None), P("shard"), P(("rep", "shard"), None)),
        check_vma=False,
    )
```

```python
import functools

import jax
import jax.numpy as jnp
from jax import lax
from jax.experimental import pallas as pl
from jax.experimental.pallas import tpu as pltpu
from jax.sharding import PartitionSpec as P

SCALE = 72.0
EPS = 1e-06
CHUNKS = 4
PIECES = 2
LOW = 2
CORES = 2
QUAD = 4
GROUP = 4
BAND = 8
F32 = jnp.float32
BF16 = jnp.bfloat16
NT = (((1,), (1,)), ((), ()))
TN = (((0,), (0,)), ((), ()))


def iota(shape, axis):
    return lax.broadcasted_iota(jnp.int32, shape, axis)


def push(src, dst, send, recv, device):
    return pltpu.make_async_remote_copy(
        src_ref=src,
        dst_ref=dst,
        send_sem=send,
        recv_sem=recv,
        device_id=device,
        device_id_type=pl.DeviceIdType.MESH,
    )


def kernel(
    reps,
    shards,
    per_target,
    ids_ref,
    q_ref,
    table_ref,
    gq_ref,
    grad_ref,
    ids_in,
    ids_plane,
    minus,
    plus,
    stage,
    onehot_t,
    arrived,
    query_unit,
    query_norm,
    query_bf,
    cand_unit,
    cand_norm,
    cand_bf,
    weights,
    coef,
    back,
    came,
    local,
    parts,
    gathered,
    ids_send,
    ids_recv,
    plane_send,
    plane_recv,
    ring_send,
    minus_recv,
    plus_recv,
    rows_send,
    rows_recv,
    back_send,
    back_recv,
    part_send,
    part_recv,
    full_send,
    full_recv,
):
    me = lax.axis_index("shard")
    rep = lax.axis_index("rep")
    per_peer = came.shape[2]
    uniq, width = table_ref.shape
    tokens = query_bf.shape[0]
    depth = shards // QUAD
    bands = depth // 2
    band_rows = BAND * per_peer
    lanes = 128
    per_pack = lanes // per_peer
    span = width // CHUNKS
    slice_rows = uniq // reps
    columns = width // GROUP
    members = GROUP * QUAD
    piece = uniq // PIECES

    z = me // CORES % depth
    my_quad = me // (CORES * depth) * CORES + me % CORES
    long = reps // LOW
    pair = rep % long // 2 * 2
    my_slice = rep // long * 2 + rep % 2
    my_place = my_slice * QUAD + my_quad

    def shard_at(quad, level):
        return quad // CORES * (CORES * depth) + level * CORES + quad % CORES

    def member(place):
        part = place // QUAD
        return {"rep": part // 2 * long + pair + part % 2, "shard": shard_at(place % QUAD, z)}

    def to_shards(body):
        def step(k, carry):
            body(lax.rem(me + k, shards))
            return carry

        lax.fori_loop(1, shards, step, 0)

    def to_reps(body):
        def step(k, carry):
            body(lax.rem(rep + k, reps))
            return carry

        lax.fori_loop(1, reps, step, 0)

    def to_members(body):
        def step(k, carry):
            body(lax.rem(my_place + k, members))
            return carry

        lax.fori_loop(1, members, step, 0)

    barrier = pltpu.get_barrier_semaphore()

    def hello(device):
        pl.semaphore_signal(
            barrier, inc=1, device_id=device, device_id_type=pl.DeviceIdType.MESH
        )

    def hello_member(place):
        @pl.when((place // QUAD != my_slice) & (place % QUAD != my_quad))
        def _():
            hello(member(place))

    to_shards(lambda p: hello({"shard": p}))
    to_reps(lambda p: hello({"rep": p}))
    to_members(hello_member)
    mine = pl.ds(pl.multiple_of(my_slice * columns, columns), columns)
    plus[0] = table_ref[:, mine].astype(BF16)
    pl.semaphore_wait(barrier, shards + reps - 2 + (GROUP - 1) * (QUAD - 1))

    up = {"shard": shard_at(my_quad, lax.rem(z + 1, depth))}
    down = {"shard": shard_at(my_quad, lax.rem(z + depth - 1, depth))}

    def rows_of(h):
        return pl.ds(h * piece, piece)

    def climb(src, step, h):
        return push(src, minus.at[step, rows_of(h)], ring_send, minus_recv.at[step, h], up)

    def sink(src, step, h):
        return push(src, plus.at[step, rows_of(h)], ring_send, plus_recv.at[step, h], down)

    for h in range(PIECES):
        climb(plus.at[0, rows_of(h)], 0, h).start()
        sink(plus.at[0, rows_of(h)], 1, h).start()
    to_members(
        lambda p: push(
            ids_ref.at[lax.rem(p, QUAD)],
            ids_plane.at[my_place],
            plane_send,
            plane_recv,
            member(p),
        ).start()
    )
    ids_plane[my_place] = ids_ref[my_quad]
    to_shards(
        lambda p: push(
            ids_ref.at[p // (CORES * depth) * CORES + p % CORES, p // CORES % depth],
            ids_in.at[me],
            ids_send,
            ids_recv,
            {"shard": p},
        ).start()
    )
    ids_in[me] = ids_ref[my_quad, z]

    values = q_ref[...].astype(F32)
    norm = jnp.sqrt(jnp.sum(values * values, axis=-1, keepdims=True) + EPS)
    unit = values / norm
    query_norm[...] = norm
    query_unit[...] = unit
    query_bf[...] = unit.astype(BF16)

    others = pl.ds(0, members - 1)
    push(ids_plane.at[others], ids_plane.at[others], plane_send, plane_recv, up).wait()

    def serve(band, half, table, level):
        which = iota((1, lanes), 1) // per_peer
        tall = []
        for pack in range(members // per_pack):
            row = ids_plane[pack * per_pack, level]
            for j in range(1, per_pack):
                row = jnp.where(which == j, ids_plane[pack * per_pack + j, level], row)
            tall.append(jnp.transpose(jnp.broadcast_to(row, (lanes, lanes))))
        column = jnp.concatenate(tall, axis=0)
        column = jnp.concatenate([column] * (uniq // lanes), axis=1)
        onehot = jnp.where(iota((members * per_peer, uniq), 1) == column, 1.0, 0.0).astype(BF16)
        rows = jnp.dot(onehot, table[...], preferred_element_type=F32).astype(BF16)
        stage[band, :, half] = rows.reshape(members, per_peer, columns)

    def gather(band, carry):
        for h in range(PIECES):
            step = climb(minus.at[band, rows_of(h)], band, h)
            step.wait_recv()

            @pl.when(band < bands - 1)
            def _():
                climb(minus.at[band, rows_of(h)], band + 1, h).start()

        for h in range(PIECES):

            @pl.when(band < bands - 1)
            def _():
                sink(plus.at[band + 1, rows_of(h)], band + 1, h).wait_recv()

            @pl.when(band < bands - 2)
            def _():
                sink(plus.at[band + 1, rows_of(h)], band + 2, h).start()

        serve(band, 0, minus.at[band], lax.rem(z + depth - band - 1, depth))
        serve(band, 1, plus.at[band], lax.rem(z + band, depth))
        there = arrived.at[band, my_slice, my_quad]
        to_members(
            lambda p: push(
                stage.at[band, p], there, rows_send, rows_recv.at[band], member(p)
            ).start()
        )
        pltpu.make_async_copy(stage.at[band, my_place], there, rows_recv.at[band]).start()
        return carry

    lax.fori_loop(0, bands, gather, 0)

    def score(band, total):
        push(arrived.at[band], arrived.at[band], rows_send, rows_recv.at[band], up).wait_recv()
        values = jnp.concatenate(
            [arrived[band, part].reshape(band_rows, columns) for part in range(GROUP)], axis=1
        ).astype(F32)
        norm = jnp.sqrt(jnp.sum(values * values, axis=-1, keepdims=True) + EPS)
        unit = values / norm
        unit_bf = unit.astype(BF16)
        cand_norm[band] = norm
        cand_unit[band] = unit
        cand_bf[band] = unit_bf
        scores = lax.dot_general(unit_bf, query_bf[...], NT, preferred_element_type=F32) * SCALE
        weight = jnp.exp(scores)
        weights[band] = weight
        return total + jnp.sum(weight, axis=0, keepdims=True)

    total = lax.fori_loop(0, bands, score, jnp.zeros((1, tokens), F32))
    share = 1.0 / total

    def owner_of(band, entry):
        level = z + depth - band - 1 if entry % 2 == 0 else z + band
        return shard_at(entry // 2, lax.rem(level, depth))

    def send_back(chunk, band, entry):
        peer = owner_of(band, entry)

        @pl.when(peer != me)
        def _():
            push(
                back.at[chunk, band, entry],
                came.at[chunk, me],
                back_send,
                back_recv.at[chunk],
                {"shard": peer},
            ).start()

    def row_grads(band, carry):
        place = iota((band_rows, 1), 0)
        quad = place // (2 * per_peer)
        level = jnp.where(place // per_peer % 2 == 1, z + band, z + depth - band - 1)
        level = jnp.where(level >= depth, level - depth, level)
        slot = place % per_peer
        target = jnp.where(slot < per_target, shard_at(quad, level) * per_target + slot, -1)
        label = jnp.where(iota((band_rows, tokens), 1) == target, 1.0, 0.0)
        coef_band = (weights[band] * share - label).astype(BF16)
        coef[band] = coef_band
        grad = jnp.dot(coef_band, query_bf[...], preferred_element_type=F32) * SCALE
        unit = cand_unit[band]
        grad = (grad - unit * jnp.sum(unit * grad, axis=-1, keepdims=True)) / cand_norm[band]
        grad = grad.astype(BF16)
        for chunk in range(CHUNKS):
            back[chunk, band] = grad[:, chunk * span : (chunk + 1) * span].reshape(
                BAND, per_peer, span
            )
        for entry in range(BAND):
            send_back(0, band, entry)
        return carry

    lax.fori_loop(0, bands, row_grads, 0)
    for chunk in range(1, CHUNKS):

        def later(band, carry):
            for entry in range(BAND):
                send_back(chunk, band, entry)
            return carry

        lax.fori_loop(0, bands, later, 0)
    for chunk in range(CHUNKS):
        pltpu.make_async_copy(
            back.at[chunk, 0, 2 * my_quad + 1], came.at[chunk, me], back_recv.at[chunk]
        ).start()

    others = pl.ds(0, shards - 1)
    push(ids_in.at[others], ids_in.at[others], ids_send, ids_recv, up).wait()

    def mark(block, carry):
        which = iota((1, lanes), 1) // per_peer
        flat = []
        for pack in range(band_rows // lanes):
            first = block * BAND + pack * per_pack
            row = ids_in[first]
            for j in range(1, per_pack):
                row = jnp.where(which == j, ids_in[first + j], row)
            flat.append(row)
        row = jnp.concatenate(flat, axis=1)
        onehot_t[block] = jnp.where(iota((uniq, band_rows), 0) == row, 1.0, 0.0).astype(BF16)
        return carry

    lax.fori_loop(0, bands, mark, 0)

    tile = 256 if tokens % 256 == 0 else 128

    def query_grads(i, carry):
        at = pl.ds(pl.multiple_of(i * tile, tile), tile)
        grad = jnp.zeros((tile, width), F32)
        for band in range(bands):
            grad += lax.dot_general(
                coef[band, :, at], cand_bf[band], TN, preferred_element_type=F32
            )
        grad = grad * SCALE
        unit = query_unit[at]
        gq_ref[at] = (grad - unit * jnp.sum(unit * grad, axis=-1, keepdims=True)) / query_norm[at]
        return carry

    lax.fori_loop(0, tokens // tile, query_grads, 0)

    def reduce_chunk(chunk):
        push(
            came.at[chunk], came.at[chunk], back_send, back_recv.at[chunk], up
        ).wait_recv()
        for half in range(2):
            rows = pl.ds(half * (uniq // 2), uniq // 2)
            grad = jnp.zeros((uniq // 2, span), F32)
            for band in range(bands):
                grad += jnp.dot(
                    onehot_t[band, rows, :],
                    came[chunk, pl.ds(band * BAND, BAND)].reshape(band_rows, span),
                    preferred_element_type=F32,
                )
            local[chunk, pl.ds(half * (reps // 2), reps // 2)] = grad.reshape(
                reps // 2, slice_rows, span
            )
        to_reps(
            lambda p: push(
                local.at[chunk, p], parts.at[chunk, rep], part_send, part_recv.at[chunk], {"rep": p}
            ).start()
        )

    def share_chunk(chunk):
        other = pl.ds(0, reps - 1)
        push(
            parts.at[chunk, other],
            parts.at[chunk, other],
            part_send,
            part_recv.at[chunk],
            up,
        ).wait_recv()
        parts[chunk, rep] = local[chunk, rep]
        gathered[chunk, rep] = jnp.sum(parts[chunk], axis=0)
        to_reps(
            lambda p: push(
                gathered.at[chunk, rep],
                gathered.at[chunk, rep],
                full_send,
                full_recv.at[chunk],
                {"rep": p},
            ).start()
        )

    def finish_chunk(chunk):
        other = pl.ds(0, reps - 1)
        push(
            gathered.at[chunk, other],
            gathered.at[chunk, other],
            full_send,
            full_recv.at[chunk],
            up,
        ).wait_recv()
        grad_ref[:, chunk * span : (chunk + 1) * span] = gathered[chunk].reshape(uniq, span)

    for chunk in range(CHUNKS):
        reduce_chunk(chunk)
        share_chunk(chunk)
    for chunk in range(CHUNKS):
        finish_chunk(chunk)

    push(plus.at[pl.ds(0, bands - 1)], plus.at[pl.ds(0, bands - 1)], ring_send, ids_recv, up).wait_send()
    push(minus, minus, ring_send, ids_recv, up).wait_send()
    other = pl.ds(0, members - 1)
    for band in range(bands):
        push(stage.at[band, other], stage.at[band, other], rows_send, ids_recv, up).wait_send()
    for chunk in range(CHUNKS):
        other = pl.ds(0, shards - 1)
        push(came.at[chunk, other], came.at[chunk, other], back_send, ids_recv, up).wait_send()
        other = pl.ds(0, reps - 1)
        push(local.at[chunk, other], local.at[chunk, other], part_send, ids_recv, up).wait_send()
        push(
            gathered.at[chunk, other], gathered.at[chunk, other], full_send, ids_recv, up
        ).wait_send()


def adam_rows(rows, first, second, grad):
    new_first = 0.9 * first + 0.1 * grad
    new_second = 0.999 * second + 0.001 * jnp.mean(grad * grad, axis=-1)
    new_rows = rows - 0.01 * new_first / (jnp.sqrt(new_second)[:, None] + 1e-08)
    return (new_rows, new_first, new_second)


def per_device(reps, shards, queries, target_ids, negative_ids, table_rows, first_moment, second_moment):
    tokens, width = queries.shape
    uniq = table_rows.shape[0]
    per_target = target_ids.shape[1]
    per_peer = per_target + negative_ids.shape[1]
    bands = shards // BAND
    band_rows = BAND * per_peer
    cands = shards * per_peer
    span = width // CHUNKS
    ids = jnp.concatenate([target_ids, negative_ids], axis=1)
    depth = shards // QUAD
    ids = jnp.tile(ids, (1, 128 // per_peer)).reshape(QUAD // CORES, depth, CORES, 128)
    ids = ids.transpose(0, 2, 1, 3).reshape(QUAD, depth, 1, 128)
    members = GROUP * QUAD
    columns = width // GROUP
    dma = pltpu.SemaphoreType.DMA
    vmem = pl.BlockSpec(memory_space=pltpu.VMEM)
    grad_queries, grad = pl.pallas_call(
        functools.partial(kernel, reps, shards, per_target),
        out_shape=(
            jax.ShapeDtypeStruct((tokens, width), F32),
            jax.ShapeDtypeStruct((uniq, width), F32),
        ),
        in_specs=[vmem] * 3,
        out_specs=(vmem, vmem),
        scratch_shapes=[
            pltpu.VMEM((shards, 1, 128), jnp.int32),
            pltpu.VMEM((members, depth, 1, 128), jnp.int32),
            pltpu.VMEM((bands, uniq, columns), BF16),
            pltpu.VMEM((bands, uniq, columns), BF16),
            pltpu.VMEM((bands, members, 2, per_peer, columns), BF16),
            pltpu.VMEM((bands, uniq, band_rows), BF16),
            pltpu.VMEM((bands, GROUP, QUAD, 2, per_peer, columns), BF16),
            pltpu.VMEM((tokens, width), F32),
            pltpu.VMEM((tokens, 1), F32),
            pltpu.VMEM((tokens, width), BF16),
            pltpu.VMEM((bands, band_rows, width), F32),
            pltpu.VMEM((bands, band_rows, 1), F32),
            pltpu.VMEM((bands, band_rows, width), BF16),
            pltpu.VMEM((bands, band_rows, tokens), F32),
            pltpu.VMEM((bands, band_rows, tokens), BF16),
            pltpu.VMEM((CHUNKS, bands, BAND, per_peer, span), BF16),
            pltpu.VMEM((CHUNKS, shards, per_peer, span), BF16),
            pltpu.VMEM((CHUNKS, reps, uniq // reps, span), F32),
            pltpu.VMEM((CHUNKS, reps, uniq // reps, span), F32),
            pltpu.VMEM((CHUNKS, reps, uniq // reps, span), F32),
            dma,
            dma,
            dma,
            dma,
            dma,
            dma((bands, PIECES)),
            dma((bands, PIECES)),
            dma,
            dma((bands,)),
            dma,
            dma((CHUNKS,)),
            dma,
            dma((CHUNKS,)),
            dma,
            dma((CHUNKS,)),
        ],
        compiler_params=pltpu.CompilerParams(
            collective_id=0, has_side_effects=True, vmem_limit_bytes=56 * 1024 * 1024
        ),
        cost_estimate=pl.CostEstimate(
            flops=2 * width * (3 * tokens * cands + 2 * uniq * cands),
            bytes_accessed=width * (6 * tokens + 8 * uniq),
            transcendentals=tokens * cands,
        ),
    )(ids, queries, table_rows)
    new_rows, new_first, new_second = adam_rows(table_rows, first_moment, second_moment, grad)
    return (new_rows, new_first, new_second, grad_queries)


def solution(mesh):
    return jax.shard_map(
        functools.partial(per_device, mesh.shape["rep"], mesh.shape["shard"]),
        mesh=mesh,
        in_specs=(
            P(("rep", "shard"), None),
            P(("rep", "shard"), None),
            P(("rep", "shard"), None),
            P("shard", None),
            P("shard", None),
            P("shard"),
        ),
        out_specs=(P("shard", None), P("shard", None), P("shard"), P(("rep", "shard"), None)),
        check_vma=False,
    )
```

```python
import functools

import jax
import jax.numpy as jnp
from jax import lax
from jax.experimental import pallas as pl
from jax.experimental.pallas import tpu as pltpu
from jax.sharding import PartitionSpec as P

SCALE = 72.0
EPS = 1e-06
CHUNKS = 4
PIECES = 2
STAGED = 3
LOW = 2
CORES = 2
QUAD = 4
GROUP = 4
BAND = 8
F32 = jnp.float32
BF16 = jnp.bfloat16
NT = (((1,), (1,)), ((), ()))
TN = (((0,), (0,)), ((), ()))


def iota(shape, axis):
    return lax.broadcasted_iota(jnp.int32, shape, axis)


def push(src, dst, send, recv, device):
    return pltpu.make_async_remote_copy(
        src_ref=src,
        dst_ref=dst,
        send_sem=send,
        recv_sem=recv,
        device_id=device,
        device_id_type=pl.DeviceIdType.MESH,
    )


def kernel(
    reps,
    shards,
    per_target,
    targets_ref,
    negatives_ref,
    q_ref,
    table_ref,
    gq_out,
    grad_out,
    square_ref,
    ids_ref,
    gq_ref,
    out_sem,
    ids_in,
    ids_plane,
    minus,
    plus,
    stage,
    onehot_t,
    arrived,
    query_unit,
    query_norm,
    query_bf,
    cand_unit,
    cand_norm,
    cand_bf,
    weights,
    coef,
    back,
    came,
    local,
    parts,
    gathered,
    ids_send,
    ids_recv,
    plane_send,
    plane_recv,
    ring_send,
    minus_recv,
    plus_recv,
    rows_send,
    rows_recv,
    back_send,
    back_recv,
    part_send,
    part_recv,
    full_send,
    full_recv,
    crossed,
    cross_send,
    cross_recv,
    half_recv,
):
    me = lax.axis_index("shard")
    rep = lax.axis_index("rep")
    per_peer = came.shape[2]
    uniq, width = table_ref.shape
    tokens = query_bf.shape[0]
    depth = shards // QUAD
    bands = depth // 2
    band_rows = BAND * per_peer
    lanes = 128
    per_pack = lanes // per_peer
    span = width // CHUNKS
    slice_rows = uniq // reps
    columns = width // GROUP
    members = GROUP * QUAD
    piece = uniq // PIECES

    z = me // CORES % depth
    my_quad = me // (CORES * depth) * CORES + me % CORES
    long = reps // LOW
    pair = rep % long // 2 * 2
    my_slice = rep // long * 2 + rep % 2
    my_place = my_slice * QUAD + my_quad

    def shard_at(quad, level):
        return quad // CORES * (CORES * depth) + level * CORES + quad % CORES

    def member(place):
        part = place // QUAD
        return {"rep": part // 2 * long + pair + part % 2, "shard": shard_at(place % QUAD, z)}

    def to_shards(body):
        def step(k, carry):
            body(lax.rem(me + k, shards))
            return carry

        lax.fori_loop(1, shards, step, 0)

    def to_reps(body):
        def step(k, carry):
            body(lax.rem(rep + k, reps))
            return carry

        lax.fori_loop(1, reps, step, 0)

    def to_members(body):
        def step(k, carry):
            body(lax.rem(my_place + k, members))
            return carry

        lax.fori_loop(1, members, step, 0)

    barrier = pltpu.get_barrier_semaphore()

    def hello(device):
        pl.semaphore_signal(
            barrier, inc=1, device_id=device, device_id_type=pl.DeviceIdType.MESH
        )

    def hello_member(place):
        @pl.when((place // QUAD != my_slice) & (place % QUAD != my_quad))
        def _():
            hello(member(place))

    to_shards(lambda p: hello({"shard": p}))
    to_reps(lambda p: hello({"rep": p}))
    to_members(hello_member)
    asked = jnp.concatenate([targets_ref[...], negatives_ref[...]] * per_pack, axis=0)
    blank = jnp.zeros((lanes, lanes - shards), jnp.int32)
    asked = jnp.transpose(jnp.concatenate([asked, blank], axis=1))
    for owner in range(shards):
        quad = owner // (CORES * depth) * CORES + owner % CORES
        ids_ref[quad, owner // CORES % depth] = asked[owner : owner + 1]
    mine = pl.ds(pl.multiple_of(my_slice * columns, columns), columns)
    plus[0] = table_ref[:, mine].astype(BF16)
    values = q_ref[...].astype(F32)
    norm = jnp.sqrt(jnp.sum(values * values, axis=-1, keepdims=True) + EPS)
    unit = values / norm
    query_norm[...] = norm
    query_unit[...] = unit
    query_bf[...] = unit.astype(BF16)
    pl.semaphore_wait(barrier, shards + reps - 2 + (GROUP - 1) * (QUAD - 1))

    up = {"shard": shard_at(my_quad, lax.rem(z + 1, depth))}
    down = {"shard": shard_at(my_quad, lax.rem(z + depth - 1, depth))}

    def rows_of(h):
        return pl.ds(h * piece, piece)

    def climb(src, step, h):
        return push(src, minus.at[step, rows_of(h)], ring_send, minus_recv.at[step, h], up)

    def sink(src, step, h):
        return push(src, plus.at[step, rows_of(h)], ring_send, plus_recv.at[step, h], down)

    for h in range(PIECES):
        climb(plus.at[0, rows_of(h)], 0, h).start()
        sink(plus.at[0, rows_of(h)], 1, h).start()
    to_members(
        lambda p: push(
            ids_ref.at[lax.rem(p, QUAD)],
            ids_plane.at[my_place],
            plane_send,
            plane_recv,
            member(p),
        ).start()
    )
    ids_plane[my_place] = ids_ref[my_quad]
    def serve(band, half, table, level):
        which = iota((1, lanes), 1) // per_peer
        tall = []
        for pack in range(members // per_pack):
            row = ids_plane[pack * per_pack, level]
            for j in range(1, per_pack):
                row = jnp.where(which == j, ids_plane[pack * per_pack + j, level], row)
            tall.append(jnp.transpose(jnp.broadcast_to(row, (lanes, lanes))))
        column = jnp.concatenate(tall, axis=0)
        column = jnp.concatenate([column] * (uniq // lanes), axis=1)
        onehot = jnp.where(iota((members * per_peer, uniq), 1) == column, 1.0, 0.0).astype(BF16)
        rows = jnp.dot(onehot, table[...], preferred_element_type=F32).astype(BF16)
        stage[band, :, half] = rows.reshape(members, per_peer, columns)

    def hop(band, h):
        @pl.when(band < bands)
        def _():
            climb(minus.at[band, rows_of(h)], band, h).wait_recv()

        @pl.when(band < bands - 1)
        def _():
            climb(minus.at[band, rows_of(h)], band + 1, h).start()
            sink(plus.at[band + 1, rows_of(h)], band + 1, h).wait_recv()

        @pl.when(band < bands - 2)
        def _():
            sink(plus.at[band + 1, rows_of(h)], band + 2, h).start()

    for h in range(PIECES):
        hop(0, h)
    others = pl.ds(0, members - 1)
    push(ids_plane.at[others], ids_plane.at[others], plane_send, plane_recv, up).wait()

    def gather(band, carry):
        serve(band, 0, minus.at[band], lax.rem(z + depth - band - 1, depth))
        for h in range(PIECES // 2):
            hop(band + 1, h)
        serve(band, 1, plus.at[band], lax.rem(z + band, depth))
        there = arrived.at[band, my_slice, my_quad]
        to_members(
            lambda p: push(
                stage.at[band, p], there, rows_send, rows_recv.at[band], member(p)
            ).start()
        )
        pltpu.make_async_copy(stage.at[band, my_place], there, rows_recv.at[band]).start()
        for h in range(PIECES // 2, PIECES):
            hop(band + 1, h)
        return carry

    lax.fori_loop(0, bands, gather, 0)
    to_shards(
        lambda p: push(
            ids_ref.at[p // (CORES * depth) * CORES + p % CORES, p // CORES % depth],
            ids_in.at[me],
            ids_send,
            ids_recv,
            {"shard": p},
        ).start()
    )
    ids_in[me] = ids_ref[my_quad, z]

    def score(band, total):
        push(arrived.at[band], arrived.at[band], rows_send, rows_recv.at[band], up).wait_recv()
        values = jnp.concatenate(
            [arrived[band, part].reshape(band_rows, columns) for part in range(GROUP)], axis=1
        ).astype(F32)
        norm = jnp.sqrt(jnp.sum(values * values, axis=-1, keepdims=True) + EPS)
        unit = values / norm
        unit_bf = unit.astype(BF16)
        cand_norm[band] = norm
        cand_unit[band] = unit
        cand_bf[band] = unit_bf
        scores = lax.dot_general(unit_bf, query_bf[...], NT, preferred_element_type=F32) * SCALE
        weight = jnp.exp(scores)
        weights[band] = weight
        return total + jnp.sum(weight, axis=0, keepdims=True)

    total = lax.fori_loop(0, bands, score, jnp.zeros((1, tokens), F32))
    share = 1.0 / total

    def owner_of(band, entry):
        level = z + depth - band - 1 if entry % 2 == 0 else z + band
        return shard_at(entry // 2, lax.rem(level, depth))

    def send_back(chunk, band, entry):
        peer = owner_of(band, entry)

        @pl.when(peer != me)
        def _():
            push(
                back.at[chunk, band, entry],
                came.at[chunk, me],
                back_send,
                back_recv.at[chunk],
                {"shard": peer},
            ).start()

    def row_grads(band, carry):
        place = iota((band_rows, 1), 0)
        quad = place // (2 * per_peer)
        level = jnp.where(place // per_peer % 2 == 1, z + band, z + depth - band - 1)
        level = jnp.where(level >= depth, level - depth, level)
        slot = place % per_peer
        target = jnp.where(slot < per_target, shard_at(quad, level) * per_target + slot, -1)
        label = jnp.where(iota((band_rows, tokens), 1) == target, 1.0, 0.0)
        coef_band = (weights[band] * share - label).astype(BF16)
        coef[band] = coef_band
        grad = jnp.dot(coef_band, query_bf[...], preferred_element_type=F32) * SCALE
        unit = cand_unit[band]
        grad = (grad - unit * jnp.sum(unit * grad, axis=-1, keepdims=True)) / cand_norm[band]
        grad = grad.astype(BF16)
        for chunk in range(CHUNKS):
            back[chunk, band] = grad[:, chunk * span : (chunk + 1) * span].reshape(
                BAND, per_peer, span
            )
        for entry in range(BAND):
            send_back(0, band, entry)
        return carry

    lax.fori_loop(0, bands, row_grads, 0)
    for chunk in range(1, CHUNKS):

        def later(band, carry):
            for entry in range(BAND):
                send_back(chunk, band, entry)
            return carry

        lax.fori_loop(0, bands, later, 0)
    for chunk in range(CHUNKS):
        pltpu.make_async_copy(
            back.at[chunk, 0, 2 * my_quad + 1], came.at[chunk, me], back_recv.at[chunk]
        ).start()

    others = pl.ds(0, shards - 1)
    push(ids_in.at[others], ids_in.at[others], ids_send, ids_recv, up).wait()

    def mark(block, carry):
        which = iota((1, lanes), 1) // per_peer
        flat = []
        for pack in range(band_rows // lanes):
            first = block * BAND + pack * per_pack
            row = ids_in[first]
            for j in range(1, per_pack):
                row = jnp.where(which == j, ids_in[first + j], row)
            flat.append(row)
        row = jnp.concatenate(flat, axis=1)
        onehot_t[block] = jnp.where(iota((uniq, band_rows), 0) == row, 1.0, 0.0).astype(BF16)
        return carry

    lax.fori_loop(0, bands, mark, 0)

    tile = 256 if tokens % 256 == 0 else 128

    def query_grads(i, carry):
        at = pl.ds(pl.multiple_of(i * tile, tile), tile)
        grad = jnp.zeros((tile, width), F32)
        for band in range(bands):
            grad += lax.dot_general(
                coef[band, :, at], cand_bf[band], TN, preferred_element_type=F32
            )
        grad = grad * SCALE
        unit = query_unit[at]
        gq_ref[at] = (grad - unit * jnp.sum(unit * grad, axis=-1, keepdims=True)) / query_norm[at]
        return carry

    lax.fori_loop(0, tokens // tile, query_grads, 0)
    pltpu.make_async_copy(gq_ref, gq_out, out_sem.at[CHUNKS]).start()

    def reduce_chunk(chunk):
        push(
            came.at[chunk], came.at[chunk], back_send, back_recv.at[chunk], up
        ).wait_recv()
        for half in range(2):
            rows = pl.ds(half * (uniq // 2), uniq // 2)
            grad = jnp.zeros((uniq // 2, span), F32)
            for band in range(bands):
                grad += jnp.dot(
                    onehot_t[band, rows, :],
                    came[chunk, pl.ds(band * BAND, BAND)].reshape(band_rows, span),
                    preferred_element_type=F32,
                )
            local[chunk, pl.ds(half * (reps // 2), reps // 2)] = grad.reshape(
                reps // 2, slice_rows, span
            )
        if chunk < STAGED:
            push(
                local.at[chunk, their_half], crossed.at[chunk], cross_send, cross_recv.at[chunk], across
            ).start()
        else:
            to_reps(
                lambda p: push(
                    local.at[chunk, p], parts.at[chunk, rep], part_send, part_recv.at[chunk], {"rep": p}
                ).start()
            )

    across = {"rep": lax.rem(rep + long, reps)}
    low = rep // long
    row = rep % long
    my_half = pl.ds(low * long, long)
    my_rows = pl.ds(pl.multiple_of(rep * slice_rows, 8), slice_rows)
    half_rows = pl.ds(pl.multiple_of(low * long * slice_rows, 8), long * slice_rows)
    their_half = pl.ds((1 - low) * long, long)

    def to_long(body):
        def step(k, carry):
            body(lax.rem(row + k, long))
            return carry

        lax.fori_loop(1, long, step, 0)

    def fold_chunk(chunk):
        push(
            crossed.at[chunk], crossed.at[chunk], cross_send, cross_recv.at[chunk], across
        ).wait_recv()
        local[chunk, my_half] += crossed[chunk]
        to_long(
            lambda p: push(
                local.at[chunk, low * long + p],
                parts.at[chunk, row],
                part_send,
                part_recv.at[chunk],
                {"rep": low * long + p},
            ).start()
        )

    def share_chunk(chunk):
        count = long if chunk < STAGED else reps
        here = row if chunk < STAGED else rep
        other = pl.ds(0, count - 1)
        push(
            parts.at[chunk, other], parts.at[chunk, other], part_send, part_recv.at[chunk], up
        ).wait_recv()
        parts[chunk, here] = local[chunk, rep]
        gathered[chunk, my_rows] = jnp.sum(parts[chunk, pl.ds(0, count)], axis=0)

        def give(p):
            push(
                gathered.at[chunk, my_rows],
                gathered.at[chunk, my_rows],
                full_send,
                full_recv.at[chunk],
                {"rep": p},
            ).start()

        if chunk < STAGED:
            to_long(lambda p: give(low * long + p))
        else:
            to_reps(give)

    def pass_chunk(chunk):
        other = pl.ds(0, (long - 1) * slice_rows)
        push(
            gathered.at[chunk, other], gathered.at[chunk, other], full_send, full_recv.at[chunk], up
        ).wait_recv()
        push(
            gathered.at[chunk, half_rows],
            gathered.at[chunk, half_rows],
            cross_send,
            half_recv.at[chunk],
            across,
        ).start()

    def to_grad(chunk):
        return pltpu.make_async_copy(
            gathered.at[chunk],
            grad_out.at[:, pl.ds(chunk * span, span)],
            out_sem.at[chunk],
        )

    def finish_chunk(chunk):
        if chunk < STAGED:
            push(
                gathered.at[chunk, half_rows],
                gathered.at[chunk, half_rows],
                cross_send,
                half_recv.at[chunk],
                across,
            ).wait_recv()
        else:
            other = pl.ds(0, (reps - 1) * slice_rows)
            push(
                gathered.at[chunk, other],
                gathered.at[chunk, other],
                full_send,
                full_recv.at[chunk],
                up,
            ).wait_recv()
        to_grad(chunk).start()
        part = gathered[chunk]
        return jnp.sum(part * part, axis=-1, keepdims=True)

    for chunk in range(CHUNKS):
        reduce_chunk(chunk)
        if 0 < chunk <= STAGED:
            pass_chunk(chunk - 1)
        if chunk < STAGED:
            fold_chunk(chunk)
        share_chunk(chunk)
    if STAGED == CHUNKS:
        pass_chunk(CHUNKS - 1)
    square = jnp.zeros((uniq, 1), F32)
    for chunk in range(CHUNKS):
        square += finish_chunk(chunk)
    square_ref[...] = jnp.broadcast_to(square, (uniq, lanes))

    push(plus.at[pl.ds(0, bands - 1)], plus.at[pl.ds(0, bands - 1)], ring_send, ids_recv, up).wait_send()
    push(minus, minus, ring_send, ids_recv, up).wait_send()
    other = pl.ds(0, members - 1)
    for band in range(bands):
        push(stage.at[band, other], stage.at[band, other], rows_send, ids_recv, up).wait_send()
    for chunk in range(CHUNKS):
        other = pl.ds(0, shards - 1)
        push(came.at[chunk, other], came.at[chunk, other], back_send, ids_recv, up).wait_send()
        other = pl.ds(0, (long if chunk < STAGED else reps) - 1)
        push(local.at[chunk, other], local.at[chunk, other], part_send, ids_recv, up).wait_send()
        other = pl.ds(0, ((long if chunk < STAGED else reps) - 1) * slice_rows)
        push(
            gathered.at[chunk, other], gathered.at[chunk, other], full_send, ids_recv, up
        ).wait_send()
        if chunk < STAGED:
            push(local.at[chunk, their_half], crossed.at[chunk], cross_send, ids_recv, up).wait_send()
            push(
                gathered.at[chunk, half_rows], gathered.at[chunk, half_rows], cross_send, ids_recv, up
            ).wait_send()
        to_grad(chunk).wait()
    pltpu.make_async_copy(gq_ref, gq_out, out_sem.at[CHUNKS]).wait()


def adam_rows(rows, first, second, grad, square):
    new_first = 0.9 * first + 0.1 * grad
    new_second = 0.999 * second + 0.001 * (square[:, 0] / grad.shape[1])
    new_rows = rows - 0.01 * new_first / (jnp.sqrt(new_second)[:, None] + 1e-08)
    return (new_rows, new_first, new_second)


def per_device(reps, shards, queries, target_ids, negative_ids, table_rows, first_moment, second_moment):
    tokens, width = queries.shape
    uniq = table_rows.shape[0]
    per_target = target_ids.shape[1]
    per_peer = per_target + negative_ids.shape[1]
    bands = shards // BAND
    band_rows = BAND * per_peer
    cands = shards * per_peer
    span = width // CHUNKS
    depth = shards // QUAD
    members = GROUP * QUAD
    columns = width // GROUP
    dma = pltpu.SemaphoreType.DMA
    vmem = pl.BlockSpec(memory_space=pltpu.VMEM)
    grad_queries, grad, square = pl.pallas_call(
        functools.partial(kernel, reps, shards, per_target),
        out_shape=(
            jax.ShapeDtypeStruct((tokens, width), F32),
            jax.ShapeDtypeStruct((uniq, width), F32),
            jax.ShapeDtypeStruct((uniq, 128), F32),
        ),
        in_specs=[vmem] * 4,
        out_specs=(pl.BlockSpec(memory_space=pl.ANY), pl.BlockSpec(memory_space=pl.ANY), vmem),
        scratch_shapes=[
            pltpu.VMEM((QUAD, depth, 1, 128), jnp.int32),
            pltpu.VMEM((tokens, width), F32),
            dma((CHUNKS + 1,)),
            pltpu.VMEM((shards, 1, 128), jnp.int32),
            pltpu.VMEM((members, depth, 1, 128), jnp.int32),
            pltpu.VMEM((bands, uniq, columns), BF16),
            pltpu.VMEM((bands, uniq, columns), BF16),
            pltpu.VMEM((bands, members, 2, per_peer, columns), BF16),
            pltpu.VMEM((bands, uniq, band_rows), BF16),
            pltpu.VMEM((bands, GROUP, QUAD, 2, per_peer, columns), BF16),
            pltpu.VMEM((tokens, width), F32),
            pltpu.VMEM((tokens, 1), F32),
            pltpu.VMEM((tokens, width), BF16),
            pltpu.VMEM((bands, band_rows, width), F32),
            pltpu.VMEM((bands, band_rows, 1), F32),
            pltpu.VMEM((bands, band_rows, width), BF16),
            pltpu.VMEM((bands, band_rows, tokens), F32),
            pltpu.VMEM((bands, band_rows, tokens), BF16),
            pltpu.VMEM((CHUNKS, bands, BAND, per_peer, span), BF16),
            pltpu.VMEM((CHUNKS, shards, per_peer, span), BF16),
            pltpu.VMEM((CHUNKS, reps, uniq // reps, span), F32),
            pltpu.VMEM((CHUNKS, reps, uniq // reps, span), F32),
            pltpu.VMEM((CHUNKS, uniq, span), F32),
            dma,
            dma,
            dma,
            dma,
            dma,
            dma((bands, PIECES)),
            dma((bands, PIECES)),
            dma,
            dma((bands,)),
            dma,
            dma((CHUNKS,)),
            dma,
            dma((CHUNKS,)),
            dma,
            dma((CHUNKS,)),
            pltpu.VMEM((CHUNKS, reps // LOW, uniq // reps, span), F32),
            dma,
            dma((CHUNKS,)),
            dma((CHUNKS,)),
        ],
        compiler_params=pltpu.CompilerParams(
            collective_id=0, has_side_effects=True, vmem_limit_bytes=56 * 1024 * 1024
        ),
        cost_estimate=pl.CostEstimate(
            flops=2 * width * (3 * tokens * cands + 2 * uniq * cands),
            bytes_accessed=width * (6 * tokens + 8 * uniq),
            transcendentals=tokens * cands,
        ),
    )(target_ids.T, negative_ids.T, queries, table_rows)
    new_rows, new_first, new_second = adam_rows(
        table_rows, first_moment, second_moment, grad, square
    )
    return (new_rows, new_first, new_second, grad_queries)


def solution(mesh):
    return jax.shard_map(
        functools.partial(per_device, mesh.shape["rep"], mesh.shape["shard"]),
        mesh=mesh,
        in_specs=(
            P(("rep", "shard"), None),
            P(("rep", "shard"), None),
            P(("rep", "shard"), None),
            P("shard", None),
            P("shard", None),
            P("shard"),
        ),
        out_specs=(P("shard", None), P("shard", None), P("shard"), P(("rep", "shard"), None)),
        check_vma=False,
    )
```

```python
import functools

import jax
import jax.numpy as jnp
from jax import lax
from jax.experimental import pallas as pl
from jax.experimental.pallas import tpu as pltpu
from jax.sharding import PartitionSpec as P

SCALE = 72.0
EPS = 1e-06
CHUNKS = 4
PIECES = 2
STAGED = 3
LOW = 2
CORES = 2
QUAD = 4
GROUP = 4
BAND = 8
F32 = jnp.float32
BF16 = jnp.bfloat16
NT = (((1,), (1,)), ((), ()))
TN = (((0,), (0,)), ((), ()))


def iota(shape, axis):
    return lax.broadcasted_iota(jnp.int32, shape, axis)


def push(src, dst, send, recv, device):
    return pltpu.make_async_remote_copy(
        src_ref=src,
        dst_ref=dst,
        send_sem=send,
        recv_sem=recv,
        device_id=device,
        device_id_type=pl.DeviceIdType.MESH,
    )


def kernel(
    reps,
    shards,
    per_target,
    targets_ref,
    negatives_ref,
    q_ref,
    table_ref,
    gq_ref,
    grad_ref,
    square_ref,
    ids_ref,
    ids_in,
    ids_plane,
    minus,
    plus,
    stage,
    onehot_t,
    arrived,
    query_unit,
    query_norm,
    query_bf,
    cand_unit,
    cand_norm,
    cand_bf,
    weights,
    coef,
    back,
    came,
    local,
    parts,
    gathered,
    ids_send,
    ids_recv,
    plane_send,
    plane_recv,
    ring_send,
    minus_recv,
    plus_recv,
    rows_send,
    rows_recv,
    back_send,
    back_recv,
    part_send,
    part_recv,
    full_send,
    full_recv,
    crossed,
    cross_send,
    cross_recv,
    half_recv,
):
    me = lax.axis_index("shard")
    rep = lax.axis_index("rep")
    per_peer = came.shape[2]
    uniq, width = table_ref.shape
    tokens = query_bf.shape[0]
    depth = shards // QUAD
    bands = depth // 2
    band_rows = BAND * per_peer
    lanes = 128
    per_pack = lanes // per_peer
    span = width // CHUNKS
    slice_rows = uniq // reps
    columns = width // GROUP
    members = GROUP * QUAD
    piece = uniq // PIECES

    z = me // CORES % depth
    my_quad = me // (CORES * depth) * CORES + me % CORES
    long = reps // LOW
    pair = rep % long // 2 * 2
    my_slice = rep // long * 2 + rep % 2
    my_place = my_slice * QUAD + my_quad

    def shard_at(quad, level):
        return quad // CORES * (CORES * depth) + level * CORES + quad % CORES

    def member(place):
        part = place // QUAD
        return {"rep": part // 2 * long + pair + part % 2, "shard": shard_at(place % QUAD, z)}

    def to_shards(body):
        def step(k, carry):
            body(lax.rem(me + k, shards))
            return carry

        lax.fori_loop(1, shards, step, 0)

    def to_reps(body):
        def step(k, carry):
            body(lax.rem(rep + k, reps))
            return carry

        lax.fori_loop(1, reps, step, 0)

    def to_members(body):
        def step(k, carry):
            body(lax.rem(my_place + k, members))
            return carry

        lax.fori_loop(1, members, step, 0)

    barrier = pltpu.get_barrier_semaphore()

    def hello(device):
        pl.semaphore_signal(
            barrier, inc=1, device_id=device, device_id_type=pl.DeviceIdType.MESH
        )

    def hello_member(place):
        @pl.when((place // QUAD != my_slice) & (place % QUAD != my_quad))
        def _():
            hello(member(place))

    to_shards(lambda p: hello({"shard": p}))
    to_reps(lambda p: hello({"rep": p}))
    to_members(hello_member)
    asked = jnp.concatenate([targets_ref[...], negatives_ref[...]] * per_pack, axis=0)
    blank = jnp.zeros((lanes, lanes - shards), jnp.int32)
    asked = jnp.transpose(jnp.concatenate([asked, blank], axis=1))
    for owner in range(shards):
        quad = owner // (CORES * depth) * CORES + owner % CORES
        ids_ref[quad, owner // CORES % depth] = asked[owner : owner + 1]
    mine = pl.ds(pl.multiple_of(my_slice * columns, columns), columns)
    plus[0] = table_ref[:, mine].astype(BF16)
    values = q_ref[...].astype(F32)
    norm = jnp.sqrt(jnp.sum(values * values, axis=-1, keepdims=True) + EPS)
    unit = values / norm
    query_norm[...] = norm
    query_unit[...] = unit
    query_bf[...] = unit.astype(BF16)
    pl.semaphore_wait(barrier, shards + reps - 2 + (GROUP - 1) * (QUAD - 1))

    up = {"shard": shard_at(my_quad, lax.rem(z + 1, depth))}
    down = {"shard": shard_at(my_quad, lax.rem(z + depth - 1, depth))}

    def rows_of(h):
        return pl.ds(h * piece, piece)

    def climb(src, step, h):
        return push(src, minus.at[step, rows_of(h)], ring_send, minus_recv.at[step, h], up)

    def sink(src, step, h):
        return push(src, plus.at[step, rows_of(h)], ring_send, plus_recv.at[step, h], down)

    for h in range(PIECES):
        climb(plus.at[0, rows_of(h)], 0, h).start()
        sink(plus.at[0, rows_of(h)], 1, h).start()
    to_members(
        lambda p: push(
            ids_ref.at[lax.rem(p, QUAD)],
            ids_plane.at[my_place],
            plane_send,
            plane_recv,
            member(p),
        ).start()
    )
    ids_plane[my_place] = ids_ref[my_quad]
    def serve(band, half, table, level):
        which = iota((1, lanes), 1) // per_peer
        tall = []
        for pack in range(members // per_pack):
            row = ids_plane[pack * per_pack, level]
            for j in range(1, per_pack):
                row = jnp.where(which == j, ids_plane[pack * per_pack + j, level], row)
            tall.append(jnp.transpose(jnp.broadcast_to(row, (lanes, lanes))))
        column = jnp.concatenate(tall, axis=0)
        column = jnp.concatenate([column] * (uniq // lanes), axis=1)
        onehot = jnp.where(iota((members * per_peer, uniq), 1) == column, 1.0, 0.0).astype(BF16)
        rows = jnp.dot(onehot, table[...], preferred_element_type=F32).astype(BF16)
        stage[band, :, half] = rows.reshape(members, per_peer, columns)

    def hop(band, h):
        @pl.when(band < bands)
        def _():
            climb(minus.at[band, rows_of(h)], band, h).wait_recv()

        @pl.when(band < bands - 1)
        def _():
            climb(minus.at[band, rows_of(h)], band + 1, h).start()
            sink(plus.at[band + 1, rows_of(h)], band + 1, h).wait_recv()

        @pl.when(band < bands - 2)
        def _():
            sink(plus.at[band + 1, rows_of(h)], band + 2, h).start()

    for h in range(PIECES):
        hop(0, h)
    others = pl.ds(0, members - 1)
    push(ids_plane.at[others], ids_plane.at[others], plane_send, plane_recv, up).wait()

    def gather(band, carry):
        serve(band, 0, minus.at[band], lax.rem(z + depth - band - 1, depth))
        for h in range(PIECES // 2):
            hop(band + 1, h)
        serve(band, 1, plus.at[band], lax.rem(z + band, depth))
        there = arrived.at[band, my_slice, my_quad]
        to_members(
            lambda p: push(
                stage.at[band, p], there, rows_send, rows_recv.at[band], member(p)
            ).start()
        )
        pltpu.make_async_copy(stage.at[band, my_place], there, rows_recv.at[band]).start()
        for h in range(PIECES // 2, PIECES):
            hop(band + 1, h)
        return carry

    lax.fori_loop(0, bands, gather, 0)
    to_shards(
        lambda p: push(
            ids_ref.at[p // (CORES * depth) * CORES + p % CORES, p // CORES % depth],
            ids_in.at[me],
            ids_send,
            ids_recv,
            {"shard": p},
        ).start()
    )
    ids_in[me] = ids_ref[my_quad, z]

    def score(band, total):
        push(arrived.at[band], arrived.at[band], rows_send, rows_recv.at[band], up).wait_recv()
        values = jnp.concatenate(
            [arrived[band, part].reshape(band_rows, columns) for part in range(GROUP)], axis=1
        ).astype(F32)
        norm = jnp.sqrt(jnp.sum(values * values, axis=-1, keepdims=True) + EPS)
        unit = values / norm
        unit_bf = unit.astype(BF16)
        cand_norm[band] = norm
        cand_unit[band] = unit
        cand_bf[band] = unit_bf
        scores = lax.dot_general(unit_bf, query_bf[...], NT, preferred_element_type=F32) * SCALE
        weight = jnp.exp(scores)
        weights[band] = weight
        return total + jnp.sum(weight, axis=0, keepdims=True)

    total = lax.fori_loop(0, bands, score, jnp.zeros((1, tokens), F32))
    share = 1.0 / total

    def owner_of(band, entry):
        level = z + depth - band - 1 if entry % 2 == 0 else z + band
        return shard_at(entry // 2, lax.rem(level, depth))

    def send_back(chunk, band, entry):
        peer = owner_of(band, entry)

        @pl.when(peer != me)
        def _():
            push(
                back.at[chunk, band, entry],
                came.at[chunk, me],
                back_send,
                back_recv.at[chunk],
                {"shard": peer},
            ).start()

    def row_grads(turn, carry):
        band = bands - 1 - turn
        place = iota((band_rows, 1), 0)
        quad = place // (2 * per_peer)
        level = jnp.where(place // per_peer % 2 == 1, z + band, z + depth - band - 1)
        level = jnp.where(level >= depth, level - depth, level)
        slot = place % per_peer
        target = jnp.where(slot < per_target, shard_at(quad, level) * per_target + slot, -1)
        label = jnp.where(iota((band_rows, tokens), 1) == target, 1.0, 0.0)
        coef_band = (weights[band] * share - label).astype(BF16)
        coef[band] = coef_band
        grad = jnp.dot(coef_band, query_bf[...], preferred_element_type=F32) * SCALE
        unit = cand_unit[band]
        grad = (grad - unit * jnp.sum(unit * grad, axis=-1, keepdims=True)) / cand_norm[band]
        grad = grad.astype(BF16)
        for chunk in range(CHUNKS):
            back[chunk, band] = grad[:, chunk * span : (chunk + 1) * span].reshape(
                BAND, per_peer, span
            )
        for entry in range(BAND):
            send_back(0, band, entry)
        return carry

    lax.fori_loop(0, bands, row_grads, 0)
    for chunk in range(1, CHUNKS):

        def later(turn, carry):
            band = bands - 1 - turn
            for entry in range(BAND):
                send_back(chunk, band, entry)
            return carry

        lax.fori_loop(0, bands, later, 0)
    for chunk in range(CHUNKS):
        pltpu.make_async_copy(
            back.at[chunk, 0, 2 * my_quad + 1], came.at[chunk, me], back_recv.at[chunk]
        ).start()

    others = pl.ds(0, shards - 1)
    push(ids_in.at[others], ids_in.at[others], ids_send, ids_recv, up).wait()

    def mark(block, carry):
        which = iota((1, lanes), 1) // per_peer
        flat = []
        for pack in range(band_rows // lanes):
            first = block * BAND + pack * per_pack
            row = ids_in[first]
            for j in range(1, per_pack):
                row = jnp.where(which == j, ids_in[first + j], row)
            flat.append(row)
        row = jnp.concatenate(flat, axis=1)
        onehot_t[block] = jnp.where(iota((uniq, band_rows), 0) == row, 1.0, 0.0).astype(BF16)
        return carry

    lax.fori_loop(0, bands, mark, 0)

    tile = 256 if tokens % 256 == 0 else 128

    def query_grads(i, carry):
        at = pl.ds(pl.multiple_of(i * tile, tile), tile)
        grad = jnp.zeros((tile, width), F32)
        for band in range(bands):
            grad += lax.dot_general(
                coef[band, :, at], cand_bf[band], TN, preferred_element_type=F32
            )
        grad = grad * SCALE
        unit = query_unit[at]
        gq_ref[at] = (grad - unit * jnp.sum(unit * grad, axis=-1, keepdims=True)) / query_norm[at]
        return carry

    lax.fori_loop(0, tokens // tile, query_grads, 0)

    def reduce_chunk(chunk):
        push(
            came.at[chunk], came.at[chunk], back_send, back_recv.at[chunk], up
        ).wait_recv()
        for half in range(2):
            rows = pl.ds(half * (uniq // 2), uniq // 2)
            grad = jnp.zeros((uniq // 2, span), F32)
            for band in range(bands):
                grad += jnp.dot(
                    onehot_t[band, rows, :],
                    came[chunk, pl.ds(band * BAND, BAND)].reshape(band_rows, span),
                    preferred_element_type=F32,
                )
            local[chunk, pl.ds(half * (reps // 2), reps // 2)] = grad.reshape(
                reps // 2, slice_rows, span
            )
        if chunk < STAGED:
            push(
                local.at[chunk, their_half], crossed.at[chunk], cross_send, cross_recv.at[chunk], across
            ).start()
        else:
            to_reps(
                lambda p: push(
                    local.at[chunk, p], parts.at[chunk, rep], part_send, part_recv.at[chunk], {"rep": p}
                ).start()
            )

    across = {"rep": lax.rem(rep + long, reps)}
    low = rep // long
    row = rep % long
    my_half = pl.ds(low * long, long)
    my_rows = pl.ds(pl.multiple_of(rep * slice_rows, 8), slice_rows)
    half_rows = pl.ds(pl.multiple_of(low * long * slice_rows, 8), long * slice_rows)
    their_half = pl.ds((1 - low) * long, long)

    def to_long(body):
        def step(k, carry):
            body(lax.rem(row + k, long))
            return carry

        lax.fori_loop(1, long, step, 0)

    def fold_chunk(chunk):
        push(
            crossed.at[chunk], crossed.at[chunk], cross_send, cross_recv.at[chunk], across
        ).wait_recv()
        local[chunk, my_half] += crossed[chunk]
        to_long(
            lambda p: push(
                local.at[chunk, low * long + p],
                parts.at[chunk, row],
                part_send,
                part_recv.at[chunk],
                {"rep": low * long + p},
            ).start()
        )

    def share_chunk(chunk):
        count = long if chunk < STAGED else reps
        here = row if chunk < STAGED else rep
        other = pl.ds(0, count - 1)
        push(
            parts.at[chunk, other], parts.at[chunk, other], part_send, part_recv.at[chunk], up
        ).wait_recv()
        parts[chunk, here] = local[chunk, rep]
        gathered[chunk, my_rows] = jnp.sum(parts[chunk, pl.ds(0, count)], axis=0)

        def give(p):
            push(
                gathered.at[chunk, my_rows],
                gathered.at[chunk, my_rows],
                full_send,
                full_recv.at[chunk],
                {"rep": p},
            ).start()

        if chunk < STAGED:
            to_long(lambda p: give(low * long + p))
        else:
            to_reps(give)

    def pass_chunk(chunk):
        other = pl.ds(0, (long - 1) * slice_rows)
        push(
            gathered.at[chunk, other], gathered.at[chunk, other], full_send, full_recv.at[chunk], up
        ).wait_recv()
        push(
            gathered.at[chunk, half_rows],
            gathered.at[chunk, half_rows],
            cross_send,
            half_recv.at[chunk],
            across,
        ).start()

    def finish_chunk(chunk):
        if chunk < STAGED:
            push(
                gathered.at[chunk, half_rows],
                gathered.at[chunk, half_rows],
                cross_send,
                half_recv.at[chunk],
                across,
            ).wait_recv()
        else:
            other = pl.ds(0, (reps - 1) * slice_rows)
            push(
                gathered.at[chunk, other],
                gathered.at[chunk, other],
                full_send,
                full_recv.at[chunk],
                up,
            ).wait_recv()
        part = gathered[chunk]
        grad_ref[:, chunk * span : (chunk + 1) * span] = part
        return jnp.sum(part * part, axis=-1, keepdims=True)

    for chunk in range(CHUNKS):
        reduce_chunk(chunk)
        if 0 < chunk <= STAGED:
            pass_chunk(chunk - 1)
        if chunk < STAGED:
            fold_chunk(chunk)
        share_chunk(chunk)
    if STAGED == CHUNKS:
        pass_chunk(CHUNKS - 1)
    square = jnp.zeros((uniq, 1), F32)
    for chunk in range(CHUNKS):
        square += finish_chunk(chunk)
    square_ref[...] = jnp.broadcast_to(square, (uniq, lanes))

    push(plus.at[pl.ds(0, bands - 1)], plus.at[pl.ds(0, bands - 1)], ring_send, ids_recv, up).wait_send()
    push(minus, minus, ring_send, ids_recv, up).wait_send()
    other = pl.ds(0, members - 1)
    for band in range(bands):
        push(stage.at[band, other], stage.at[band, other], rows_send, ids_recv, up).wait_send()
    for chunk in range(CHUNKS):
        other = pl.ds(0, shards - 1)
        push(came.at[chunk, other], came.at[chunk, other], back_send, ids_recv, up).wait_send()
        other = pl.ds(0, (long if chunk < STAGED else reps) - 1)
        push(local.at[chunk, other], local.at[chunk, other], part_send, ids_recv, up).wait_send()
        other = pl.ds(0, ((long if chunk < STAGED else reps) - 1) * slice_rows)
        push(
            gathered.at[chunk, other], gathered.at[chunk, other], full_send, ids_recv, up
        ).wait_send()
        if chunk < STAGED:
            push(local.at[chunk, their_half], crossed.at[chunk], cross_send, ids_recv, up).wait_send()
            push(
                gathered.at[chunk, half_rows], gathered.at[chunk, half_rows], cross_send, ids_recv, up
            ).wait_send()


def adam_kernel(rows_ref, first_ref, second_ref, grad_ref, square_ref, new_rows, new_first, new_second):
    lanes = square_ref.shape[1]
    width = grad_ref.shape[1]
    at = pl.program_id(0)
    second = jnp.transpose(jnp.broadcast_to(second_ref[at], (lanes, lanes)))
    second = 0.999 * second + 0.001 * (square_ref[...] / width)
    new_second[at] = jnp.transpose(second)[0:1]
    root = jnp.sqrt(second) + 1e-08
    for k in range(width // lanes):
        part = slice(k * lanes, (k + 1) * lanes)
        first = 0.9 * first_ref[:, part] + 0.1 * grad_ref[:, part]
        new_first[:, part] = first
        new_rows[:, part] = rows_ref[:, part] - 0.01 * first / root


def adam_rows(rows, first, second, grad, square):
    uniq, width = rows.shape
    lanes = square.shape[1]
    blocks = uniq // lanes
    block = pl.BlockSpec((lanes, width), lambda i: (i, 0))
    line = pl.BlockSpec((blocks, 1, lanes), lambda i: (0, 0, 0))
    table = jax.ShapeDtypeStruct((uniq, width), F32)
    new_rows, new_first, new_second = pl.pallas_call(
        adam_kernel,
        grid=(blocks,),
        out_shape=(table, table, jax.ShapeDtypeStruct((blocks, 1, lanes), F32)),
        in_specs=[block, block, line, block, pl.BlockSpec((lanes, lanes), lambda i: (i, 0))],
        out_specs=(block, block, line),
        cost_estimate=pl.CostEstimate(
            flops=8 * uniq * width, bytes_accessed=20 * uniq * width, transcendentals=uniq
        ),
    )(rows, first, second.reshape(blocks, 1, lanes), grad, square)
    return (new_rows, new_first, new_second.reshape(uniq))


def per_device(reps, shards, queries, target_ids, negative_ids, table_rows, first_moment, second_moment):
    tokens, width = queries.shape
    uniq = table_rows.shape[0]
    per_target = target_ids.shape[1]
    per_peer = per_target + negative_ids.shape[1]
    bands = shards // BAND
    band_rows = BAND * per_peer
    cands = shards * per_peer
    span = width // CHUNKS
    depth = shards // QUAD
    members = GROUP * QUAD
    columns = width // GROUP
    dma = pltpu.SemaphoreType.DMA
    vmem = pl.BlockSpec(memory_space=pltpu.VMEM)
    grad_queries, grad, square = pl.pallas_call(
        functools.partial(kernel, reps, shards, per_target),
        out_shape=(
            jax.ShapeDtypeStruct((tokens, width), F32),
            jax.ShapeDtypeStruct((uniq, width), F32),
            jax.ShapeDtypeStruct((uniq, 128), F32),
        ),
        in_specs=[vmem] * 4,
        out_specs=(vmem, vmem, vmem),
        scratch_shapes=[
            pltpu.VMEM((QUAD, depth, 1, 128), jnp.int32),
            pltpu.VMEM((shards, 1, 128), jnp.int32),
            pltpu.VMEM((members, depth, 1, 128), jnp.int32),
            pltpu.VMEM((bands, uniq, columns), BF16),
            pltpu.VMEM((bands, uniq, columns), BF16),
            pltpu.VMEM((bands, members, 2, per_peer, columns), BF16),
            pltpu.VMEM((bands, uniq, band_rows), BF16),
            pltpu.VMEM((bands, GROUP, QUAD, 2, per_peer, columns), BF16),
            pltpu.VMEM((tokens, width), F32),
            pltpu.VMEM((tokens, 1), F32),
            pltpu.VMEM((tokens, width), BF16),
            pltpu.VMEM((bands, band_rows, width), F32),
            pltpu.VMEM((bands, band_rows, 1), F32),
            pltpu.VMEM((bands, band_rows, width), BF16),
            pltpu.VMEM((bands, band_rows, tokens), F32),
            pltpu.VMEM((bands, band_rows, tokens), BF16),
            pltpu.VMEM((CHUNKS, bands, BAND, per_peer, span), BF16),
            pltpu.VMEM((CHUNKS, shards, per_peer, span), BF16),
            pltpu.VMEM((CHUNKS, reps, uniq // reps, span), F32),
            pltpu.VMEM((CHUNKS, reps, uniq // reps, span), F32),
            pltpu.VMEM((CHUNKS, uniq, span), F32),
            dma,
            dma,
            dma,
            dma,
            dma,
            dma((bands, PIECES)),
            dma((bands, PIECES)),
            dma,
            dma((bands,)),
            dma,
            dma((CHUNKS,)),
            dma,
            dma((CHUNKS,)),
            dma,
            dma((CHUNKS,)),
            pltpu.VMEM((CHUNKS, reps // LOW, uniq // reps, span), F32),
            dma,
            dma((CHUNKS,)),
            dma((CHUNKS,)),
        ],
        compiler_params=pltpu.CompilerParams(
            collective_id=0, has_side_effects=True, vmem_limit_bytes=56 * 1024 * 1024
        ),
        cost_estimate=pl.CostEstimate(
            flops=2 * width * (3 * tokens * cands + 2 * uniq * cands),
            bytes_accessed=width * (6 * tokens + 8 * uniq),
            transcendentals=tokens * cands,
        ),
    )(target_ids.T, negative_ids.T, queries, table_rows)
    new_rows, new_first, new_second = adam_rows(
        table_rows, first_moment, second_moment, grad, square
    )
    return (new_rows, new_first, new_second, grad_queries)


def solution(mesh):
    return jax.shard_map(
        functools.partial(per_device, mesh.shape["rep"], mesh.shape["shard"]),
        mesh=mesh,
        in_specs=(
            P(("rep", "shard"), None),
            P(("rep", "shard"), None),
            P(("rep", "shard"), None),
            P("shard", None),
            P("shard", None),
            P("shard"),
        ),
        out_specs=(P("shard", None), P("shard", None), P("shard"), P(("rep", "shard"), None)),
        check_vma=False,
    )
```

```python
import functools

import jax
import jax.numpy as jnp
from jax import lax
from jax.experimental import pallas as pl
from jax.experimental.pallas import tpu as pltpu
from jax.sharding import PartitionSpec as P

SCALE = 72.0
EPS = 1e-06
CHUNKS = 4
PIECES = 2
STAGED = 3
STEPS = 2
LOW = 2
CORES = 2
QUAD = 4
GROUP = 4
BAND = 8
F32 = jnp.float32
BF16 = jnp.bfloat16
NT = (((1,), (1,)), ((), ()))
TN = (((0,), (0,)), ((), ()))


def iota(shape, axis):
    return lax.broadcasted_iota(jnp.int32, shape, axis)


def push(src, dst, send, recv, device):
    return pltpu.make_async_remote_copy(
        src_ref=src,
        dst_ref=dst,
        send_sem=send,
        recv_sem=recv,
        device_id=device,
        device_id_type=pl.DeviceIdType.MESH,
    )


def kernel(
    reps,
    shards,
    per_target,
    targets_ref,
    negatives_ref,
    q_ref,
    table_ref,
    gq_ref,
    grad_ref,
    square_ref,
    ids_ref,
    ids_in,
    ids_plane,
    minus,
    plus,
    stage,
    onehot_t,
    arrived,
    query_unit,
    query_norm,
    query_bf,
    cand_unit,
    cand_norm,
    cand_bf,
    weights,
    coef,
    back,
    came,
    local,
    parts,
    gathered,
    ids_send,
    ids_recv,
    plane_send,
    plane_recv,
    ring_send,
    minus_recv,
    plus_recv,
    rows_send,
    rows_recv,
    back_send,
    back_recv,
    part_send,
    part_recv,
    full_send,
    full_recv,
    crossed,
    cross_send,
    cross_recv,
    half_recv,
):
    me = lax.axis_index("shard")
    rep = lax.axis_index("rep")
    per_peer = came.shape[2]
    uniq, width = table_ref.shape
    tokens = query_bf.shape[0]
    depth = shards // QUAD
    bands = depth // 2
    band_rows = BAND * per_peer
    lanes = 128
    per_pack = lanes // per_peer
    span = width // CHUNKS
    slice_rows = uniq // reps
    columns = width // GROUP
    members = GROUP * QUAD
    piece = uniq // PIECES

    z = me // CORES % depth
    my_quad = me // (CORES * depth) * CORES + me % CORES
    long = reps // LOW
    pair = rep % long // 2 * 2
    my_slice = rep // long * 2 + rep % 2
    my_place = my_slice * QUAD + my_quad

    def shard_at(quad, level):
        return quad // CORES * (CORES * depth) + level * CORES + quad % CORES

    def member(place):
        part = place // QUAD
        return {"rep": part // 2 * long + pair + part % 2, "shard": shard_at(place % QUAD, z)}

    def to_shards(body):
        def step(k, carry):
            body(lax.rem(me + k, shards))
            return carry

        lax.fori_loop(1, shards, step, 0)

    def to_reps(body):
        def step(k, carry):
            body(lax.rem(rep + k, reps))
            return carry

        lax.fori_loop(1, reps, step, 0)

    def to_members(body):
        def step(k, carry):
            body(lax.rem(my_place + k, members))
            return carry

        lax.fori_loop(1, members, step, 0)

    barrier = pltpu.get_barrier_semaphore()

    def hello(device):
        pl.semaphore_signal(
            barrier, inc=1, device_id=device, device_id_type=pl.DeviceIdType.MESH
        )

    def hello_member(place):
        @pl.when((place // QUAD != my_slice) & (place % QUAD != my_quad))
        def _():
            hello(member(place))

    to_shards(lambda p: hello({"shard": p}))
    to_reps(lambda p: hello({"rep": p}))
    to_members(hello_member)
    asked = jnp.concatenate([targets_ref[...], negatives_ref[...]] * per_pack, axis=0)
    blank = jnp.zeros((lanes, lanes - shards), jnp.int32)
    asked = jnp.transpose(jnp.concatenate([asked, blank], axis=1))
    for owner in range(shards):
        quad = owner // (CORES * depth) * CORES + owner % CORES
        ids_ref[quad, owner // CORES % depth] = asked[owner : owner + 1]
    mine = pl.ds(pl.multiple_of(my_slice * columns, columns), columns)
    plus[0] = table_ref[:, mine].astype(BF16)
    values = q_ref[...].astype(F32)
    norm = jnp.sqrt(jnp.sum(values * values, axis=-1, keepdims=True) + EPS)
    unit = values / norm
    query_norm[...] = norm
    query_unit[...] = unit
    query_bf[...] = unit.astype(BF16)
    pl.semaphore_wait(barrier, shards + reps - 2 + (GROUP - 1) * (QUAD - 1))

    up = {"shard": shard_at(my_quad, lax.rem(z + 1, depth))}
    down = {"shard": shard_at(my_quad, lax.rem(z + depth - 1, depth))}

    def rows_of(h):
        return pl.ds(h * piece, piece)

    def climb(src, step, h):
        return push(src, minus.at[step, rows_of(h)], ring_send, minus_recv.at[step, h], up)

    def sink(src, step, h):
        return push(src, plus.at[step, rows_of(h)], ring_send, plus_recv.at[step, h], down)

    for h in range(PIECES):
        climb(plus.at[0, rows_of(h)], 0, h).start()
        sink(plus.at[0, rows_of(h)], 1, h).start()
    to_members(
        lambda p: push(
            ids_ref.at[lax.rem(p, QUAD)],
            ids_plane.at[my_place],
            plane_send,
            plane_recv,
            member(p),
        ).start()
    )
    ids_plane[my_place] = ids_ref[my_quad]
    def serve(band, half, table, level):
        which = iota((1, lanes), 1) // per_peer
        tall = []
        for pack in range(members // per_pack):
            row = ids_plane[pack * per_pack, level]
            for j in range(1, per_pack):
                row = jnp.where(which == j, ids_plane[pack * per_pack + j, level], row)
            tall.append(jnp.transpose(jnp.broadcast_to(row, (lanes, lanes))))
        column = jnp.concatenate(tall, axis=0)
        column = jnp.concatenate([column] * (uniq // lanes), axis=1)
        onehot = jnp.where(iota((members * per_peer, uniq), 1) == column, 1.0, 0.0).astype(BF16)
        rows = jnp.dot(onehot, table[...], preferred_element_type=F32).astype(BF16)
        stage[band, :, half] = rows.reshape(members, per_peer, columns)

    def hop(band, h):
        @pl.when(band < bands)
        def _():
            climb(minus.at[band, rows_of(h)], band, h).wait_recv()

        @pl.when(band < bands - 1)
        def _():
            climb(minus.at[band, rows_of(h)], band + 1, h).start()
            sink(plus.at[band + 1, rows_of(h)], band + 1, h).wait_recv()

        @pl.when(band < bands - 2)
        def _():
            sink(plus.at[band + 1, rows_of(h)], band + 2, h).start()

    for h in range(PIECES):
        hop(0, h)
    others = pl.ds(0, members - 1)
    push(ids_plane.at[others], ids_plane.at[others], plane_send, plane_recv, up).wait()

    def gather(band, carry):
        serve(band, 0, minus.at[band], lax.rem(z + depth - band - 1, depth))
        for h in range(PIECES // 2):
            hop(band + 1, h)
        serve(band, 1, plus.at[band], lax.rem(z + band, depth))
        there = arrived.at[band, my_slice, my_quad]
        to_members(
            lambda p: push(
                stage.at[band, p], there, rows_send, rows_recv.at[band], member(p)
            ).start()
        )
        pltpu.make_async_copy(stage.at[band, my_place], there, rows_recv.at[band]).start()
        for h in range(PIECES // 2, PIECES):
            hop(band + 1, h)
        return carry

    lax.fori_loop(0, bands, gather, 0)
    to_shards(
        lambda p: push(
            ids_ref.at[p // (CORES * depth) * CORES + p % CORES, p // CORES % depth],
            ids_in.at[me],
            ids_send,
            ids_recv,
            {"shard": p},
        ).start()
    )
    ids_in[me] = ids_ref[my_quad, z]

    def score(band, total):
        push(arrived.at[band], arrived.at[band], rows_send, rows_recv.at[band], up).wait_recv()
        values = jnp.concatenate(
            [arrived[band, part].reshape(band_rows, columns) for part in range(GROUP)], axis=1
        ).astype(F32)
        norm = jnp.sqrt(jnp.sum(values * values, axis=-1, keepdims=True) + EPS)
        unit = values / norm
        unit_bf = unit.astype(BF16)
        cand_norm[band] = norm
        cand_unit[band] = unit
        cand_bf[band] = unit_bf
        scores = lax.dot_general(unit_bf, query_bf[...], NT, preferred_element_type=F32) * SCALE
        weight = jnp.exp(scores)
        weights[band] = weight
        return total + jnp.sum(weight, axis=0, keepdims=True)

    total = lax.fori_loop(0, bands, score, jnp.zeros((1, tokens), F32))
    share = 1.0 / total

    def owner_of(band, entry):
        level = z + depth - band - 1 if entry % 2 == 0 else z + band
        return shard_at(entry // 2, lax.rem(level, depth))

    def send_back(chunk, band, entry):
        peer = owner_of(band, entry)

        @pl.when(peer != me)
        def _():
            push(
                back.at[chunk, band, entry],
                came.at[chunk, me],
                back_send,
                back_recv.at[chunk],
                {"shard": peer},
            ).start()

    def row_grads(turn, carry):
        band = bands - 1 - turn
        place = iota((band_rows, 1), 0)
        quad = place // (2 * per_peer)
        level = jnp.where(place // per_peer % 2 == 1, z + band, z + depth - band - 1)
        level = jnp.where(level >= depth, level - depth, level)
        slot = place % per_peer
        target = jnp.where(slot < per_target, shard_at(quad, level) * per_target + slot, -1)
        label = jnp.where(iota((band_rows, tokens), 1) == target, 1.0, 0.0)
        coef_band = (weights[band] * share - label).astype(BF16)
        coef[band] = coef_band
        grad = jnp.dot(coef_band, query_bf[...], preferred_element_type=F32) * SCALE
        unit = cand_unit[band]
        grad = (grad - unit * jnp.sum(unit * grad, axis=-1, keepdims=True)) / cand_norm[band]
        grad = grad.astype(BF16)
        for chunk in range(CHUNKS):
            back[chunk, band] = grad[:, chunk * span : (chunk + 1) * span].reshape(
                BAND, per_peer, span
            )
        for entry in range(BAND):
            send_back(0, band, entry)
        return carry

    lax.fori_loop(0, bands, row_grads, 0)
    for chunk in range(1, CHUNKS):

        def later(turn, carry):
            band = bands - 1 - turn
            for entry in range(BAND):
                send_back(chunk, band, entry)
            return carry

        lax.fori_loop(0, bands, later, 0)
    for chunk in range(CHUNKS):
        pltpu.make_async_copy(
            back.at[chunk, 0, 2 * my_quad + 1], came.at[chunk, me], back_recv.at[chunk]
        ).start()

    others = pl.ds(0, shards - 1)
    push(ids_in.at[others], ids_in.at[others], ids_send, ids_recv, up).wait()

    def mark(block, carry):
        which = iota((1, lanes), 1) // per_peer
        flat = []
        for pack in range(band_rows // lanes):
            first = block * BAND + pack * per_pack
            row = ids_in[first]
            for j in range(1, per_pack):
                row = jnp.where(which == j, ids_in[first + j], row)
            flat.append(row)
        row = jnp.concatenate(flat, axis=1)
        onehot_t[block] = jnp.where(iota((uniq, band_rows), 0) == row, 1.0, 0.0).astype(BF16)
        return carry

    lax.fori_loop(0, bands, mark, 0)

    tile = 256 if tokens % 256 == 0 else 128

    def query_grads(i, carry):
        at = pl.ds(pl.multiple_of(i * tile, tile), tile)
        grad = jnp.zeros((tile, width), F32)
        for band in range(bands):
            grad += lax.dot_general(
                coef[band, :, at], cand_bf[band], TN, preferred_element_type=F32
            )
        grad = grad * SCALE
        unit = query_unit[at]
        gq_ref[at] = (grad - unit * jnp.sum(unit * grad, axis=-1, keepdims=True)) / query_norm[at]
        return carry

    lax.fori_loop(0, tokens // tile, query_grads, 0)

    def reduce_chunk(chunk):
        push(
            came.at[chunk], came.at[chunk], back_send, back_recv.at[chunk], up
        ).wait_recv()
        for half in range(2):
            rows = pl.ds(half * (uniq // 2), uniq // 2)
            grad = jnp.zeros((uniq // 2, span), F32)
            for band in range(bands):
                grad += jnp.dot(
                    onehot_t[band, rows, :],
                    came[chunk, pl.ds(band * BAND, BAND)].reshape(band_rows, span),
                    preferred_element_type=F32,
                )
            local[chunk, pl.ds(half * (reps // 2), reps // 2)] = grad.reshape(
                reps // 2, slice_rows, span
            )
        if chunk < STAGED:
            push(
                local.at[chunk, their_half], crossed.at[chunk], cross_send, cross_recv.at[chunk], across
            ).start()
        else:
            to_reps(
                lambda p: push(
                    local.at[chunk, p], parts.at[chunk, rep], part_send, part_recv.at[chunk], {"rep": p}
                ).start()
            )

    across = {"rep": lax.rem(rep + long, reps)}
    low = rep // long
    row = rep % long
    my_half = pl.ds(low * long, long)
    my_rows = pl.ds(pl.multiple_of(rep * slice_rows, 8), slice_rows)
    half_rows = pl.ds(pl.multiple_of(low * long * slice_rows, 8), long * slice_rows)
    their_half = pl.ds((1 - low) * long, long)

    def to_long(body):
        def step(k, carry):
            body(lax.rem(row + k, long))
            return carry

        lax.fori_loop(1, long, step, 0)

    def fold_chunk(chunk):
        push(
            crossed.at[chunk], crossed.at[chunk], cross_send, cross_recv.at[chunk], across
        ).wait_recv()
        local[chunk, my_half] += crossed[chunk]
        to_long(
            lambda p: push(
                local.at[chunk, low * long + p],
                parts.at[chunk, row],
                part_send,
                part_recv.at[chunk],
                {"rep": low * long + p},
            ).start()
        )

    def share_chunk(chunk):
        count = long if chunk < STAGED else reps
        here = row if chunk < STAGED else rep
        other = pl.ds(0, count - 1)
        push(
            parts.at[chunk, other], parts.at[chunk, other], part_send, part_recv.at[chunk], up
        ).wait_recv()
        parts[chunk, here] = local[chunk, rep]
        gathered[chunk, my_rows] = jnp.sum(parts[chunk, pl.ds(0, count)], axis=0)

        def give(p):
            push(
                gathered.at[chunk, my_rows],
                gathered.at[chunk, my_rows],
                full_send,
                full_recv.at[chunk],
                {"rep": p},
            ).start()

        if chunk < STAGED:
            to_long(lambda p: give(low * long + p))
        else:
            to_reps(give)

    def pass_chunk(chunk):
        other = pl.ds(0, (long - 1) * slice_rows)
        push(
            gathered.at[chunk, other], gathered.at[chunk, other], full_send, full_recv.at[chunk], up
        ).wait_recv()
        push(
            gathered.at[chunk, half_rows],
            gathered.at[chunk, half_rows],
            cross_send,
            half_recv.at[chunk],
            across,
        ).start()

    def finish_chunk(chunk):
        if chunk < STAGED:
            push(
                gathered.at[chunk, half_rows],
                gathered.at[chunk, half_rows],
                cross_send,
                half_recv.at[chunk],
                across,
            ).wait_recv()
        else:
            other = pl.ds(0, (reps - 1) * slice_rows)
            push(
                gathered.at[chunk, other],
                gathered.at[chunk, other],
                full_send,
                full_recv.at[chunk],
                up,
            ).wait_recv()
        part = gathered[chunk]
        grad_ref[:, chunk * span : (chunk + 1) * span] = part
        return jnp.sum(part * part, axis=-1, keepdims=True)

    for chunk in range(CHUNKS):
        reduce_chunk(chunk)
        if 0 < chunk <= STAGED:
            pass_chunk(chunk - 1)
        if chunk < STAGED:
            fold_chunk(chunk)
        share_chunk(chunk)
    if STAGED == CHUNKS:
        pass_chunk(CHUNKS - 1)
    square = jnp.zeros((uniq, 1), F32)
    for chunk in range(CHUNKS):
        square += finish_chunk(chunk)
    square_ref[...] = jnp.broadcast_to(square, (uniq, lanes))

    push(plus.at[pl.ds(0, bands - 1)], plus.at[pl.ds(0, bands - 1)], ring_send, ids_recv, up).wait_send()
    push(minus, minus, ring_send, ids_recv, up).wait_send()
    other = pl.ds(0, members - 1)
    for band in range(bands):
        push(stage.at[band, other], stage.at[band, other], rows_send, ids_recv, up).wait_send()
    for chunk in range(CHUNKS):
        other = pl.ds(0, shards - 1)
        push(came.at[chunk, other], came.at[chunk, other], back_send, ids_recv, up).wait_send()
        other = pl.ds(0, (long if chunk < STAGED else reps) - 1)
        push(local.at[chunk, other], local.at[chunk, other], part_send, ids_recv, up).wait_send()
        other = pl.ds(0, ((long if chunk < STAGED else reps) - 1) * slice_rows)
        push(
            gathered.at[chunk, other], gathered.at[chunk, other], full_send, ids_recv, up
        ).wait_send()
        if chunk < STAGED:
            push(local.at[chunk, their_half], crossed.at[chunk], cross_send, ids_recv, up).wait_send()
            push(
                gathered.at[chunk, half_rows], gathered.at[chunk, half_rows], cross_send, ids_recv, up
            ).wait_send()


def adam_kernel(rows_ref, first_ref, second_ref, grad_ref, square_ref, new_rows, new_first, new_second):
    rows, lanes = square_ref.shape
    width = grad_ref.shape[1]
    for block in range(rows // lanes):
        at = pl.program_id(0) * (rows // lanes) + block
        here = slice(block * lanes, (block + 1) * lanes)
        second = jnp.transpose(jnp.broadcast_to(second_ref[at], (lanes, lanes)))
        second = 0.999 * second + 0.001 * (square_ref[here] / width)
        new_second[at] = jnp.transpose(second)[0:1]
        root = jnp.sqrt(second) + 1e-08
        for k in range(width // lanes):
            part = slice(k * lanes, (k + 1) * lanes)
            first = 0.9 * first_ref[here, part] + 0.1 * grad_ref[here, part]
            new_first[here, part] = first
            new_rows[here, part] = rows_ref[here, part] - 0.01 * first / root


def adam_rows(rows, first, second, grad, square):
    uniq, width = rows.shape
    lanes = square.shape[1]
    blocks = uniq // lanes
    tall = uniq // STEPS
    block = pl.BlockSpec((tall, width), lambda i: (i, 0))
    line = pl.BlockSpec((blocks, 1, lanes), lambda i: (0, 0, 0))
    table = jax.ShapeDtypeStruct((uniq, width), F32)
    new_rows, new_first, new_second = pl.pallas_call(
        adam_kernel,
        grid=(STEPS,),
        out_shape=(table, table, jax.ShapeDtypeStruct((blocks, 1, lanes), F32)),
        in_specs=[block, block, line, block, pl.BlockSpec((tall, lanes), lambda i: (i, 0))],
        out_specs=(block, block, line),
        compiler_params=pltpu.CompilerParams(vmem_limit_bytes=32 * 1024 * 1024),
        cost_estimate=pl.CostEstimate(
            flops=8 * uniq * width, bytes_accessed=20 * uniq * width, transcendentals=uniq
        ),
    )(rows, first, second.reshape(blocks, 1, lanes), grad, square)
    return (new_rows, new_first, new_second.reshape(uniq))


def per_device(reps, shards, queries, target_ids, negative_ids, table_rows, first_moment, second_moment):
    tokens, width = queries.shape
    uniq = table_rows.shape[0]
    per_target = target_ids.shape[1]
    per_peer = per_target + negative_ids.shape[1]
    bands = shards // BAND
    band_rows = BAND * per_peer
    cands = shards * per_peer
    span = width // CHUNKS
    depth = shards // QUAD
    members = GROUP * QUAD
    columns = width // GROUP
    dma = pltpu.SemaphoreType.DMA
    vmem = pl.BlockSpec(memory_space=pltpu.VMEM)
    grad_queries, grad, square = pl.pallas_call(
        functools.partial(kernel, reps, shards, per_target),
        out_shape=(
            jax.ShapeDtypeStruct((tokens, width), F32),
            jax.ShapeDtypeStruct((uniq, width), F32),
            jax.ShapeDtypeStruct((uniq, 128), F32),
        ),
        in_specs=[vmem] * 4,
        out_specs=(vmem, vmem, vmem),
        scratch_shapes=[
            pltpu.VMEM((QUAD, depth, 1, 128), jnp.int32),
            pltpu.VMEM((shards, 1, 128), jnp.int32),
            pltpu.VMEM((members, depth, 1, 128), jnp.int32),
            pltpu.VMEM((bands, uniq, columns), BF16),
            pltpu.VMEM((bands, uniq, columns), BF16),
            pltpu.VMEM((bands, members, 2, per_peer, columns), BF16),
            pltpu.VMEM((bands, uniq, band_rows), BF16),
            pltpu.VMEM((bands, GROUP, QUAD, 2, per_peer, columns), BF16),
            pltpu.VMEM((tokens, width), F32),
            pltpu.VMEM((tokens, 1), F32),
            pltpu.VMEM((tokens, width), BF16),
            pltpu.VMEM((bands, band_rows, width), F32),
            pltpu.VMEM((bands, band_rows, 1), F32),
            pltpu.VMEM((bands, band_rows, width), BF16),
            pltpu.VMEM((bands, band_rows, tokens), F32),
            pltpu.VMEM((bands, band_rows, tokens), BF16),
            pltpu.VMEM((CHUNKS, bands, BAND, per_peer, span), BF16),
            pltpu.VMEM((CHUNKS, shards, per_peer, span), BF16),
            pltpu.VMEM((CHUNKS, reps, uniq // reps, span), F32),
            pltpu.VMEM((CHUNKS, reps, uniq // reps, span), F32),
            pltpu.VMEM((CHUNKS, uniq, span), F32),
            dma,
            dma,
            dma,
            dma,
            dma,
            dma((bands, PIECES)),
            dma((bands, PIECES)),
            dma,
            dma((bands,)),
            dma,
            dma((CHUNKS,)),
            dma,
            dma((CHUNKS,)),
            dma,
            dma((CHUNKS,)),
            pltpu.VMEM((CHUNKS, reps // LOW, uniq // reps, span), F32),
            dma,
            dma((CHUNKS,)),
            dma((CHUNKS,)),
        ],
        compiler_params=pltpu.CompilerParams(
            collective_id=0, has_side_effects=True, vmem_limit_bytes=56 * 1024 * 1024
        ),
        cost_estimate=pl.CostEstimate(
            flops=2 * width * (3 * tokens * cands + 2 * uniq * cands),
            bytes_accessed=width * (6 * tokens + 8 * uniq),
            transcendentals=tokens * cands,
        ),
    )(target_ids.T, negative_ids.T, queries, table_rows)
    new_rows, new_first, new_second = adam_rows(
        table_rows, first_moment, second_moment, grad, square
    )
    return (new_rows, new_first, new_second, grad_queries)


def solution(mesh):
    return jax.shard_map(
        functools.partial(per_device, mesh.shape["rep"], mesh.shape["shard"]),
        mesh=mesh,
        in_specs=(
            P(("rep", "shard"), None),
            P(("rep", "shard"), None),
            P(("rep", "shard"), None),
            P("shard", None),
            P("shard", None),
            P("shard"),
        ),
        out_specs=(P("shard", None), P("shard", None), P("shard"), P(("rep", "shard"), None)),
        check_vma=False,
    )
```
